512 devices in a mesh: group: 64 (over z, y_lo, core), mp: 8 (over x, y_hi).
Axes of the slice: x: 4, y: 4 (y_hi: 2, y_lo: 2; y = y_hi * 2 + y_lo), z: 16, core: 2. Of those that a mesh axis runs over, the one named last changes fastest.
Arguments:
- tokens: bfloat16 [3, 4096, 4096], P(None, 'group'), may hold values from -600 to 600
- neighbour_ids: int32 [64, 3, 128], P('group'), may hold values from 0 to 65535, as said below
- group_document: int32 [3, 64], replicated, may hold values from 0 to 15, never falling along the last dimension, each value on 1 to 8 neighbouring positions
- embed_table: bfloat16 [65536, 4096], P('group', 'mp'), may hold values from -6 to 6
- w_query: bfloat16 [4096, 2048], P('group', 'mp'), may hold values from -0.09375 to 0.09375
- w_key: bfloat16 [4096, 2048], P('group', 'mp'), may hold values from -0.09375 to 0.09375
- w_value: bfloat16 [4096, 2048], P('group', 'mp'), may hold values from -0.375 to 0.375
- attended_grad: bfloat16 [3, 4096, 2048], P(None, 'group', 'mp'), may hold values from -6 to 6
Outputs:
- attended: bfloat16 [3, 4096, 2048], P(None, 'group', 'mp')
- token_grad: bfloat16 [3, 4096, 4096], P(None, 'group')
The draws below stay inside these ranges and needn't reach their ends.
Inputs may be any that keep to these rules, and one draw needn't show every extreme that they name: `neighbour_ids`: among the ids of one group, all sequences together, at most 9 fall in any one block of 1024 consecutive ids starting at a multiple of 1024; in every draw one block holds exactly 9 ids of every group. `group_document`: never falls along a sequence; a document covers 1 to 8 groups.
All inputs are finite; a program needn't handle non-finite values.
Results may differ from the reference program's by a relative error of at most 0.0065.
The reference program's roundings to bfloat16 on the way count: a program that leaves them out, or rounds other values in their place, can miss the bound.
Values may be sent and summed in bfloat16 or wider, within the bound.
No kernel may reach another device: no remote copies, remote signals or barrier semaphores. Data moves between devices by JAX's collectives and lax.ppermute only.
A program may use at most 128 MiB of HBM per device.

```python
import math
import jax
import jax.numpy as jnp
import numpy as np

D = 4096
HEADS = 16
HEAD_DIM = 128
VOCAB = 65536
GROUP_LEN = 64
SEQS = 3
NCHUNKS = 64
LENGTH = 4096
NKEYS = 128
ROWS_OWN = 1024
CAP = 9


def draw_tokens(key, part):
    key = jax.random.fold_in(key, 1)
    base_key = jax.random.fold_in(key, 0)
    normal_vals = jnp.clip(jax.random.normal(base_key, (SEQS, LENGTH, D), jnp.float32), -6.0, 6.0)
    return normal_vals.astype(jnp.bfloat16)


def draw_neighbour_ids(key, part):
    key = jax.random.fold_in(key, 2)
    full_key, score_key, shuffle_key, row_key = jax.random.split(key, 4)
    slot_total = NCHUNKS * CAP
    id_count = SEQS * NKEYS
    full_owner = jax.random.randint(full_key, (), 0, NCHUNKS)
    slot_owner = jnp.arange(slot_total, dtype=jnp.int32) // CAP
    noise_int = jax.random.randint(score_key, (NCHUNKS, slot_total), 0, 1 << 16)
    slot_score = noise_int * slot_total + jnp.arange(slot_total, dtype=jnp.int32)[None, :]
    slot_score = slot_score + jnp.where(slot_owner == full_owner, 1 << 30, 0)[None, :]
    ranked = jnp.argsort(-slot_score, axis=1)[:, :id_count]
    shuffle_int = jax.random.randint(shuffle_key, (NCHUNKS, id_count), 0, 1 << 16)
    shuffle = jnp.argsort(shuffle_int * id_count + jnp.arange(id_count, dtype=jnp.int32)[None, :], axis=1)
    ranked = jnp.take_along_axis(ranked, shuffle, axis=1)
    owner_group = (ranked // CAP).astype(jnp.int32)
    row_pick = jax.random.randint(row_key, (NCHUNKS, id_count), 0, ROWS_OWN)
    id_values = owner_group * ROWS_OWN + row_pick
    return id_values.reshape(NCHUNKS, SEQS, NKEYS).astype(jnp.int32)


def level_of(stream_key, dims, cuts, low, largest):
    def one(position, blocks):
        draws = jax.random.uniform(jax.random.fold_in(jax.random.fold_in(stream_key, 6), position), (blocks,), jnp.float32, low / len(cuts), largest / len(cuts))
        return jnp.repeat(jnp.exp(draws), dims[position] // blocks).reshape((-1,) + (1,) * (len(dims) - position - 1))

    factor_of = one(*cuts[0])
    for cut in cuts[1:]:
        factor_of = factor_of * one(*cut)
    return factor_of


def length_profile(number_of, total, reach, lean):
    portions = [(1 << 20) // math.isqrt(grade ** lean) + 1 for grade in range(2, number_of + 1)]
    surplus, given = total - reach - (number_of - 1), [1] * (number_of - 1)
    while surplus > 0:
        movable = [i for i in range(number_of - 1) if given[i] < reach]
        mass, left = sum([portions[i] for i in movable]), surplus
        for i in movable:
            extra = min(reach - given[i], max(1, left * portions[i] // mass), surplus)
            given[i] = given[i] + extra
            surplus = surplus - extra
    return np.array([reach] + given)


def uneven_parts(stream_key, amount, total, most, lean):
    if amount == 2:
        one = jax.random.randint(stream_key, (), max(1, total - most), min(most, total - 1) + 1)
        return jnp.stack([one, total - one])
    lengths = jnp.asarray(length_profile(amount, total, most, lean), jnp.int32)
    pairs = (amount - 1) // 2
    donor, sink = lengths[1:1 + 2 * pairs:2], lengths[2:2 + 2 * pairs:2]
    margin = jnp.minimum(donor - 1, most - sink)
    passed = jax.random.randint(jax.random.fold_in(stream_key, 1), (pairs,), 0, 1 << 20) % (margin + 1)
    lengths = lengths.at[1:1 + 2 * pairs:2].set(donor - passed).at[2:2 + 2 * pairs:2].set(sink + passed)
    return lengths[jax.random.permutation(jax.random.fold_in(stream_key, 2), amount)]


def centred(stream_key, shape, width, reach, pieces=(), kind=jnp.bfloat16):
    entries = width * jax.random.normal(stream_key, shape, jnp.float32)
    if pieces:
        entries = entries * level_of(stream_key, shape, pieces, -0.22, 0.18)
    return jnp.clip(entries, -reach, reach).astype(kind)


def setup_inputs(seed: int = 0) -> dict:
    streams_of = jax.random.split(jax.random.key(seed), 9)
    return {
        "tokens": draw_tokens(jax.random.fold_in(streams_of[8], 71), 0),
        "neighbour_ids": draw_neighbour_ids(jax.random.fold_in(streams_of[8], 71), 0),
        "group_document": jax.vmap(lambda own: jnp.searchsorted(jnp.cumsum(uneven_parts(own, NCHUNKS // 4, NCHUNKS, 8, 0)), jnp.arange(NCHUNKS), side="right"))(jax.random.split(streams_of[2], SEQS)).reshape((SEQS, NCHUNKS)).astype(jnp.int32),
        "embed_table": centred(streams_of[3], (VOCAB, D), 1.0, 6.0, ((0, 64), (1, 8))),
        "w_query": centred(streams_of[4], (D, HEADS * HEAD_DIM), D ** -0.5, 0.09375, ((0, 64), (1, 8))),
        "w_key": centred(streams_of[5], (D, HEADS * HEAD_DIM), D ** -0.5, 0.09375, ((0, 64), (1, 8))),
        "w_value": centred(streams_of[6], (D, HEADS * HEAD_DIM), (D // 16) ** -0.5, 0.375, ((0, 64), (1, 8))),
        "attended_grad": centred(streams_of[7], (SEQS, LENGTH, HEADS * HEAD_DIM), 1.0, 6.0, ((1, 64), (2, 8))),
    }


def token_valid(group_document):
    last_token = jnp.arange(GROUP_LEN) == GROUP_LEN - 1
    same_doc = jnp.concatenate([jnp.zeros((SEQS, 1), dtype=bool), group_document[:, 1:] == group_document[:, :-1]], axis=1)
    return last_token[None, None, :] | same_doc[:, :, None]


def reference(tokens, neighbour_ids, group_document, embed_table, w_query, w_key, w_value, attended_grad):
    head_cols = HEADS * HEAD_DIM
    score_scale = HEAD_DIM ** -0.5
    encoded = embed_table[neighbour_ids].reshape(-1, D)
    key_own = jnp.dot(encoded, w_key, preferred_element_type=jnp.float32).astype(jnp.bfloat16)
    key_own = key_own.reshape(NCHUNKS, SEQS, NKEYS, HEADS, HEAD_DIM).transpose(1, 0, 2, 3, 4)
    value_own = jnp.dot(encoded, w_value, preferred_element_type=jnp.float32).astype(jnp.bfloat16)
    value_own = value_own.reshape(NCHUNKS, SEQS, NKEYS, HEADS, HEAD_DIM).transpose(1, 0, 2, 3, 4)
    key_prev = jnp.concatenate([jnp.zeros_like(key_own[:, :1]), key_own[:, :-1]], axis=1)
    value_prev = jnp.concatenate([jnp.zeros_like(value_own[:, :1]), value_own[:, :-1]], axis=1)
    query_act = jnp.dot(tokens.reshape(-1, D), w_query, preferred_element_type=jnp.float32).astype(jnp.bfloat16)
    query_act = query_act.reshape(SEQS, NCHUNKS, GROUP_LEN, HEADS, HEAD_DIM)
    query_f = query_act.astype(jnp.float32)
    last_token = (jnp.arange(GROUP_LEN) == GROUP_LEN - 1)[:, None]
    score_prev = jnp.einsum('sclhd,sckhd->schlk', query_f, key_prev.astype(jnp.float32)) * score_scale
    score_own = jnp.einsum('sclhd,sckhd->schlk', query_f, key_own.astype(jnp.float32)) * score_scale
    scores = jnp.where(last_token, score_own, score_prev)
    row_max = jnp.max(scores, axis=-1, keepdims=True)
    exp_scores = jnp.exp(scores - row_max)
    attn_prob = exp_scores / jnp.sum(exp_scores, axis=-1, keepdims=True)
    prob_bf = attn_prob.astype(jnp.bfloat16)
    prob_prev = jnp.where(last_token, jnp.zeros_like(prob_bf), prob_bf).astype(jnp.float32)
    prob_own = jnp.where(last_token, prob_bf, jnp.zeros_like(prob_bf)).astype(jnp.float32)
    mixed_sum = jnp.einsum('schlk,sckhd->sclhd', prob_prev, value_prev.astype(jnp.float32))
    mixed_sum = mixed_sum + jnp.einsum('schlk,sckhd->sclhd', prob_own, value_own.astype(jnp.float32))
    valid_tok = token_valid(group_document)[:, :, :, None, None]
    attended = jnp.where(valid_tok, mixed_sum, 0.0).astype(jnp.bfloat16).reshape(SEQS, LENGTH, head_cols)
    grad_in = attended_grad.reshape(SEQS, NCHUNKS, GROUP_LEN, HEADS, HEAD_DIM).astype(jnp.float32)
    grad_kept = jnp.where(valid_tok, grad_in, 0.0)
    grad_prev = jnp.einsum('sclhd,sckhd->schlk', grad_kept, value_prev.astype(jnp.float32))
    grad_own = jnp.einsum('sclhd,sckhd->schlk', grad_kept, value_own.astype(jnp.float32))
    prob_grad = jnp.where(last_token, grad_own, grad_prev)
    dscore = attn_prob * (prob_grad - jnp.sum(attn_prob * prob_grad, axis=-1, keepdims=True)) * score_scale
    dscore = dscore.astype(jnp.bfloat16)
    dscore_prev = jnp.where(last_token, jnp.zeros_like(dscore), dscore).astype(jnp.float32)
    dscore_own = jnp.where(last_token, dscore, jnp.zeros_like(dscore)).astype(jnp.float32)
    dquery = jnp.einsum('schlk,sckhd->sclhd', dscore_prev, key_prev.astype(jnp.float32))
    dquery = dquery + jnp.einsum('schlk,sckhd->sclhd', dscore_own, key_own.astype(jnp.float32))
    dquery = dquery.astype(jnp.bfloat16).reshape(-1, head_cols)
    token_grad = jnp.dot(dquery, w_query.T, preferred_element_type=jnp.float32).astype(jnp.bfloat16)
    return attended, token_grad.reshape(SEQS, LENGTH, D)
```

```python
import jax
import jax.numpy as jnp
from jax import lax
from jax.sharding import PartitionSpec as P

HEAD_DIM = 128


def gather_mp(value):
    count = lax.axis_size("mp")
    copies = jnp.broadcast_to(value[None], (count,) + value.shape)
    return lax.all_to_all(copies, "mp", split_axis=0, concat_axis=0, tiled=True)


def local(
    tokens, neighbour_ids, group_document, embed_table, w_query, w_key, w_value, attended_grad
):
    nchunk = lax.axis_size("group")
    mp_size = lax.axis_size("mp")
    group_here = lax.axis_index("group")
    seq_count, group_len, model_width = tokens.shape
    depth_rows, head_cols = w_query.shape
    local_heads = head_cols // HEAD_DIM
    score_scale = HEAD_DIM ** (-0.5)
    onward = [(g, (g + 1) % nchunk) for g in range(nchunk)]
    backward = [(g, (g - 1) % nchunk) for g in range(nchunk)]

    per = nchunk // mp_size
    spread = [
        (r * mp_size + c, (c * per + r % per) * mp_size + r // per)
        for r in range(nchunk)
        for c in range(mp_size)
    ]
    row_piece = lax.ppermute(w_query, ("group", "mp"), spread)
    weights = lax.all_gather(
        jnp.concatenate([w_key, w_value, w_query, row_piece], axis=1), "group", axis=0, tiled=True
    )
    kv_w = weights[:, : 2 * head_cols]
    query_w = weights[:, 2 * head_cols : 3 * head_cols]
    row_w = weights[:, 3 * head_cols :].reshape(mp_size, per * depth_rows, head_cols)

    last_tok, last_grad = lax.ppermute(
        (tokens[:, -1:], attended_grad[:, -1:]), "group", onward
    )
    moved_tok = jnp.concatenate([last_tok, tokens[:, :-1]], axis=1)
    moved_grad = jnp.concatenate([last_grad, attended_grad[:, :-1]], axis=1)

    flat_ids = neighbour_ids.reshape(-1)
    id_count = flat_ids.shape[0]
    key_count = id_count // seq_count
    rows_dev = embed_table.shape[0]
    capacity = max(2, 3 * id_count // (2 * nchunk))
    owner_group = flat_ids // rows_dev
    onehot = (owner_group[:, None] == jnp.arange(nchunk, dtype=jnp.int32)[None, :]).astype(
        jnp.int32
    )
    before = jnp.cumsum(onehot, axis=0) - onehot
    bucket_rank = jnp.sum(before * onehot, axis=1)
    requests = (
        jnp.zeros((nchunk, 128), jnp.int32)
        .at[owner_group, bucket_rank]
        .set(flat_ids - owner_group * rows_dev)
    )
    slot_index = lax.ppermute(owner_group * capacity + bucket_rank, "group", onward)
    asked = lax.all_to_all(requests, "group", split_axis=0, concat_axis=0, tiled=True)
    asked = jnp.roll(asked[:, :capacity], 1, axis=0)
    found_rows = embed_table[asked].reshape(nchunk, -1)
    returned = lax.all_to_all(found_rows, "group", split_axis=0, concat_axis=0, tiled=True)
    encoded = returned.reshape(nchunk * capacity, -1)[slot_index]
    blocks = gather_mp(encoded)
    block_cols = jnp.swapaxes(blocks, 0, 1).reshape(id_count, model_width)

    kv = jnp.dot(block_cols, kv_w, preferred_element_type=jnp.float32).astype(jnp.bfloat16)
    keys = kv[:, :head_cols].reshape(seq_count, key_count, local_heads, HEAD_DIM)
    values = kv[:, head_cols:].reshape(seq_count, key_count, local_heads, HEAD_DIM)
    query_act = jnp.dot(
        moved_tok.reshape(-1, model_width), query_w, preferred_element_type=jnp.float32
    )
    query_act = query_act.astype(jnp.bfloat16).reshape(seq_count, group_len, local_heads, HEAD_DIM)

    earlier = jnp.maximum(group_here - 1, 0)
    doc_here = lax.dynamic_slice_in_dim(group_document, group_here, 1, 1)[:, 0]
    doc_before = lax.dynamic_slice_in_dim(group_document, earlier, 1, 1)[:, 0]
    same_doc = (group_here >= 1) & (doc_here == doc_before)
    first = jnp.arange(group_len) == 0
    valid_tok = (first[None, :] | same_doc[:, None])[:, :, None, None]

    scores = (
        jnp.einsum("slhd,skhd->shlk", query_act, keys, preferred_element_type=jnp.float32)
        * score_scale
    )
    row_max = jnp.max(scores, axis=-1, keepdims=True)
    exp_scores = jnp.exp(scores - row_max)
    attn_prob = exp_scores / jnp.sum(exp_scores, axis=-1, keepdims=True)
    prob_bf = attn_prob.astype(jnp.bfloat16)
    mixed_sum = jnp.einsum(
        "shlk,skhd->slhd", prob_bf, values, preferred_element_type=jnp.float32
    )
    attended = (
        jnp.where(valid_tok, mixed_sum, 0.0)
        .astype(jnp.bfloat16)
        .reshape(seq_count, group_len, head_cols)
    )
    grad_in = moved_grad.reshape(seq_count, group_len, local_heads, HEAD_DIM)
    grad_kept = jnp.where(valid_tok, grad_in, jnp.zeros_like(grad_in))
    prob_grad = jnp.einsum(
        "slhd,skhd->shlk", grad_kept, values, preferred_element_type=jnp.float32
    )
    dscore = (
        attn_prob
        * (prob_grad - jnp.sum(attn_prob * prob_grad, axis=-1, keepdims=True))
        * score_scale
    ).astype(jnp.bfloat16)
    dquery = jnp.einsum("shlk,skhd->slhd", dscore, keys, preferred_element_type=jnp.float32)
    dquery = dquery.astype(jnp.bfloat16).reshape(seq_count, group_len, head_cols)

    last = lax.ppermute(
        jnp.concatenate([attended[:, :1], dquery[:, :1]], axis=-1), "group", backward
    )
    attended = jnp.concatenate([attended[:, 1:], last[:, :, :head_cols]], axis=1)
    dquery = jnp.concatenate([dquery[:, 1:], last[:, :, head_cols:]], axis=1)
    all_dquery = gather_mp(dquery.reshape(-1, head_cols))
    part = jnp.einsum(
        "ctj,cnj->tn", all_dquery, row_w, preferred_element_type=jnp.float32
    ).astype(jnp.bfloat16)
    token_grad = jnp.swapaxes(gather_mp(part), 0, 1)
    return (attended, token_grad.reshape(seq_count, group_len, model_width))


def solution(mesh):
    in_specs = (
        P(None, "group", None),
        P("group", None, None),
        P(),
        P("group", "mp"),
        P("group", "mp"),
        P("group", "mp"),
        P("group", "mp"),
        P(None, "group", "mp"),
    )
    out_specs = (P(None, "group", "mp"), P(None, "group", None))
    return jax.shard_map(local, mesh=mesh, in_specs=in_specs, out_specs=out_specs, check_vma=False)
```

```python
import functools

import jax
import jax.numpy as jnp
from jax import lax
from jax.experimental import pallas as pl
from jax.experimental.pallas import tpu as pltpu
from jax.sharding import PartitionSpec as P

HEAD_DIM = 128
BF, F32, I32 = jnp.bfloat16, jnp.float32, jnp.int32
PARAMS = pltpu.CompilerParams(vmem_limit_bytes=48 * 1024 * 1024)
NT = (((1,), (1,)), ((), ()))


def iota(shape, dim):
    return lax.broadcasted_iota(I32, shape, dim)


def dot(a, b, dims=(((1,), (0,)), ((), ()))):
    return lax.dot_general(a, b, dims, preferred_element_type=F32)


def bucket_kernel(nchunk, rows_dev, ids_ref, requests_ref, slot_ref):
    seqs, keys = ids_ref.shape
    ids = jnp.concatenate([ids_ref[s : s + 1, :] for s in range(seqs)], axis=1)
    total = seqs * keys
    owner = ids // rows_dev
    lid = ids - owner * rows_dev
    owned = (iota((nchunk, total), 0) == owner).astype(F32)
    owned_bf = owned.astype(BF)
    earlier = (iota((total, total), 0) < iota((total, total), 1)).astype(F32).astype(BF)
    rank = jnp.sum(dot(owned_bf, earlier) * owned, axis=0, keepdims=True).astype(I32)
    placed = iota((128, total), 0) == rank
    high = jnp.where(placed, lid // 32, 0).astype(F32).astype(BF)
    low = jnp.where(placed, lid % 32, 0).astype(F32).astype(BF)
    requests_ref[...] = (dot(owned_bf, high, NT) * 32.0 + dot(owned_bf, low, NT)).astype(I32)
    slot = rank * nchunk + owner
    for s in range(seqs):
        slot_ref[s : s + 1, :] = slot[:, s * keys : (s + 1) * keys]


def fetch_kernel(capacity, asked_ref, table_ref, out_ref):
    nchunk = asked_ref.shape[0]
    rows_dev, feats = table_ref.shape
    asked = pltpu.roll(asked_ref[...], 1, 0)
    lanes = iota((nchunk, rows_dev), 1)
    chosen = jnp.concatenate(
        [(asked[:, s : s + 1] == lanes).astype(F32).astype(BF) for s in range(capacity)], axis=0
    )
    found = dot(chosen, table_ref[...]).astype(BF)
    for s in range(capacity):
        out_ref[:, s * feats : (s + 1) * feats] = found[s * nchunk : (s + 1) * nchunk]


def order_kernel(capacity, slot_ref, rows_ref, out_ref):
    seqs, keys = slot_ref.shape
    nchunk = rows_ref.shape[0]
    copies, _, feats = out_ref.shape
    rows = jnp.concatenate(
        [rows_ref[:, s * feats : (s + 1) * feats] for s in range(capacity)], axis=0
    )
    slots = jnp.concatenate([slot_ref[...], jnp.zeros((8 - seqs, keys), I32)], axis=0)
    slots = slots.astype(F32).T.astype(I32)
    lanes = iota((keys, capacity * nchunk), 1)
    for s in range(seqs):
        chosen = (slots[:, s : s + 1] == lanes).astype(F32).astype(BF)
        found = dot(chosen, rows).astype(BF)
        for c in range(copies):
            out_ref[c, s * keys : (s + 1) * keys, :] = found


def interleave(core0, core1, run):
    parts = []
    for start in range(0, core0.shape[0], run):
        parts += [core0[start : start + run], core1[start : start + run]]
    return jnp.concatenate(parts, axis=0)


def attend_kernel(
    run, scal_ref, enc_ref, mine_ref, other_ref, tok_ref, last_tok_ref, grad_ref, last_grad_ref,
    att_ref, dq_ref, kv_acc, q_acc,
):
    step, steps = pl.program_id(0), pl.num_programs(0)
    seqs, length, cols = grad_ref.shape
    keys = kv_acc.shape[0] // seqs

    @pl.when(step == 0)
    def _():
        kv_acc[...] = jnp.zeros_like(kv_acc)
        q_acc[...] = jnp.zeros_like(q_acc)

    is_last = iota((length, tok_ref.shape[2]), 0) == length - 1
    tok = jnp.concatenate(
        [jnp.where(is_last, last_tok_ref[s : s + 1, :], tok_ref[s]) for s in range(seqs)], axis=0
    )

    def add(core0, core1):
        weights = interleave(core0, core1, run)
        kv_acc[...] += dot(enc_ref[0], weights[:, : 2 * cols])
        q_acc[...] += dot(tok, weights[:, 2 * cols :])

    @pl.when(scal_ref[0] == 0)
    def _():
        add(mine_ref[...], other_ref[...])

    @pl.when(scal_ref[0] != 0)
    def _():
        add(other_ref[...], mine_ref[...])

    @pl.when(step == steps - 1)
    def _():
        scale = HEAD_DIM ** (-0.5)
        last_row = iota((length, HEAD_DIM), 0) == length - 1
        for s in range(seqs):
            valid = last_row | (scal_ref[1 + s] != 0)
            for h in range(cols // HEAD_DIM):
                head = slice(h * HEAD_DIM, (h + 1) * HEAD_DIM)
                value_head = slice(cols + h * HEAD_DIM, cols + (h + 1) * HEAD_DIM)
                query = q_acc[s * length : (s + 1) * length, head].astype(BF)
                key = kv_acc[s * keys : (s + 1) * keys, head].astype(BF)
                value = kv_acc[s * keys : (s + 1) * keys, value_head].astype(BF)
                grad = jnp.where(last_row, last_grad_ref[s : s + 1, head], grad_ref[s, :, head])
                grad = jnp.where(valid, grad, jnp.zeros_like(grad))
                scores = dot(query, key, NT) * scale
                exps = jnp.exp(scores - jnp.max(scores, axis=-1, keepdims=True))
                prob = exps / jnp.sum(exps, axis=-1, keepdims=True)
                mixed = dot(prob.astype(BF), value)
                att_ref[s, :, head] = jnp.where(valid, mixed, 0.0).astype(BF)
                prob_grad = dot(grad, value, NT)
                mean = jnp.sum(prob * prob_grad, axis=-1, keepdims=True)
                dscore = (prob * (prob_grad - mean) * scale).astype(BF)
                dq_ref[s, :, head] = dot(dscore, key).astype(BF)


def return_kernel(att_ref, dq_ref, last_ref, att_out, dq_out):
    seqs, length, cols = att_ref.shape
    is_last = iota((length, cols), 0) == length - 1
    for s in range(seqs):
        att_out[s] = jnp.where(is_last, last_ref[s : s + 1, :cols], att_ref[s])
        rows = jnp.where(is_last, last_ref[s : s + 1, cols:], dq_ref[s])
        for c in range(dq_out.shape[0]):
            dq_out[c, s * length : (s + 1) * length, :] = rows


def token_kernel(run, scal_ref, dq_ref, mine_ref, other_ref, out_ref, acc):
    step, steps = pl.program_id(0), pl.num_programs(0)

    @pl.when(step == 0)
    def _():
        acc[...] = jnp.zeros_like(acc)

    @pl.when(scal_ref[0] == 0)
    def _():
        acc[...] += dot(dq_ref[0], interleave(mine_ref[...], other_ref[...], run), NT)

    @pl.when(scal_ref[0] != 0)
    def _():
        acc[...] += dot(dq_ref[0], interleave(other_ref[...], mine_ref[...], run), NT)

    @pl.when(step == steps - 1)
    def _():
        rounded = acc[...].astype(BF)
        for c in range(out_ref.shape[0]):
            out_ref[c] = rounded


def join_kernel(in_ref, out_ref):
    out_ref[...] = in_ref[0]


def local(
    tokens, neighbour_ids, group_document, embed_table, w_query, w_key, w_value, attended_grad
):
    nchunk = lax.axis_size("group")
    mp_size = lax.axis_size("mp")
    group_here = lax.axis_index("group")
    core = group_here % 2
    seqs, length, width = tokens.shape
    run, cols = w_query.shape
    keys = neighbour_ids.shape[2]
    id_count = seqs * keys
    rows_dev, feats = embed_table.shape
    capacity = max(2, 3 * id_count // (2 * nchunk))
    per = nchunk // mp_size
    onward = [(g, (g + 1) % nchunk) for g in range(nchunk)]
    backward = [(g, (g - 1) % nchunk) for g in range(nchunk)]

    def across(g):
        return g ^ 2

    def spread(turn):
        return [
            (r * mp_size + c, turn(c * per + r % per) * mp_size + r // per)
            for r in range(nchunk)
            for c in range(mp_size)
        ]

    own = jnp.concatenate([w_key, w_value, w_query], axis=1)
    near = lax.ppermute(own, "group", [(g, across(g)) for g in range(nchunk)])
    piece = lax.ppermute(w_query, ("group", "mp"), spread(lambda g: g))
    near_piece = lax.ppermute(w_query, ("group", "mp"), spread(across))
    own = jnp.concatenate([own, piece], axis=1)
    near = jnp.concatenate([near, near_piece], axis=1)
    lower = (group_here // 2) % 2 == 0
    pair = jnp.concatenate([jnp.where(lower, own, near), jnp.where(lower, near, own)], axis=0)
    mine = lax.all_gather(
        pair, "group", axis=0, tiled=True,
        axis_index_groups=[[z * 4 + r for z in range(nchunk // 4)] for r in range(4)],
    )
    other = lax.ppermute(mine, "group", [(g, g ^ 1) for g in range(nchunk)])

    last_tok, last_grad = lax.ppermute((tokens[:, -1], attended_grad[:, -1]), "group", onward)

    requests, slot = pl.pallas_call(
        functools.partial(bucket_kernel, nchunk, rows_dev),
        out_shape=[
            jax.ShapeDtypeStruct((nchunk, 128), I32),
            jax.ShapeDtypeStruct((seqs, keys), I32),
        ],
        compiler_params=PARAMS,
    )(neighbour_ids.reshape(seqs, keys))
    slot = lax.ppermute(slot, "group", onward)
    asked = lax.all_to_all(requests, "group", split_axis=0, concat_axis=0, tiled=True)
    found = pl.pallas_call(
        functools.partial(fetch_kernel, capacity),
        out_shape=jax.ShapeDtypeStruct((nchunk, capacity * feats), BF),
        compiler_params=PARAMS,
    )(asked, embed_table)
    returned = lax.all_to_all(found, "group", split_axis=0, concat_axis=0, tiled=True)
    encoded = pl.pallas_call(
        functools.partial(order_kernel, capacity),
        out_shape=jax.ShapeDtypeStruct((mp_size, id_count, feats), BF),
        compiler_params=PARAMS,
    )(slot, returned)
    encoded = lax.all_to_all(encoded, "mp", split_axis=0, concat_axis=0, tiled=True)

    earlier = jnp.maximum(group_here - 1, 0)
    doc_here = lax.dynamic_slice_in_dim(group_document, group_here, 1, 1)[:, 0]
    doc_before = lax.dynamic_slice_in_dim(group_document, earlier, 1, 1)[:, 0]
    same_doc = (group_here >= 1) & (doc_here == doc_before)
    scalars = jnp.concatenate([core[None].astype(I32), same_doc.astype(I32)])

    half = width // mp_size // 2
    whole = lambda *shape: pl.BlockSpec(shape, lambda i, s: (0,) * len(shape))
    att, dquery = pl.pallas_call(
        functools.partial(attend_kernel, run),
        grid_spec=pltpu.PrefetchScalarGridSpec(
            num_scalar_prefetch=1,
            grid=(mp_size,),
            in_specs=[
                pl.BlockSpec((1, id_count, feats), lambda i, s: (i, 0, 0)),
                pl.BlockSpec((half, 3 * cols), lambda i, s: (i, 0)),
                pl.BlockSpec((half, 3 * cols), lambda i, s: (i, 0)),
                pl.BlockSpec((seqs, length, feats), lambda i, s: (0, 0, i)),
                pl.BlockSpec((seqs, feats), lambda i, s: (0, i)),
                whole(seqs, length, cols),
                whole(seqs, cols),
            ],
            out_specs=[whole(seqs, length, cols), whole(seqs, length, cols)],
            scratch_shapes=[
                pltpu.VMEM((id_count, 2 * cols), F32),
                pltpu.VMEM((seqs * length, cols), F32),
            ],
        ),
        out_shape=[jax.ShapeDtypeStruct((seqs, length, cols), BF)] * 2,
        compiler_params=PARAMS,
    )(scalars, encoded, mine, other, tokens, last_tok, attended_grad, last_grad)

    last = lax.ppermute(
        jnp.concatenate([att[:, -1], dquery[:, -1]], axis=-1), "group", backward
    )
    attended, dquery = pl.pallas_call(
        return_kernel,
        out_shape=[
            jax.ShapeDtypeStruct((seqs, length, cols), BF),
            jax.ShapeDtypeStruct((mp_size, seqs * length, cols), BF),
        ],
        compiler_params=PARAMS,
    )(att, dquery, last)
    dquery = lax.all_to_all(dquery, "mp", split_axis=0, concat_axis=0, tiled=True)
    part = pl.pallas_call(
        functools.partial(token_kernel, run),
        grid_spec=pltpu.PrefetchScalarGridSpec(
            num_scalar_prefetch=1,
            grid=(mp_size,),
            in_specs=[
                pl.BlockSpec((1, seqs * length, cols), lambda i, s: (i, 0, 0)),
                pl.BlockSpec((half, cols), lambda i, s: (i, 3)),
                pl.BlockSpec((half, cols), lambda i, s: (i, 3)),
            ],
            out_specs=whole(mp_size, seqs * length, feats),
            scratch_shapes=[pltpu.VMEM((seqs * length, feats), F32)],
        ),
        out_shape=jax.ShapeDtypeStruct((mp_size, seqs * length, feats), BF),
        compiler_params=PARAMS,
    )(scalars, dquery, mine, other)
    part = lax.all_to_all(part, "mp", split_axis=0, concat_axis=0, tiled=True)
    token_grad = pl.pallas_call(
        join_kernel,
        grid=(mp_size,),
        in_specs=[pl.BlockSpec((1, seqs * length, feats), lambda i: (i, 0, 0))],
        out_specs=pl.BlockSpec((seqs * length, feats), lambda i: (0, i)),
        out_shape=jax.ShapeDtypeStruct((seqs * length, width), BF),
        compiler_params=PARAMS,
    )(part)
    return (attended, token_grad.reshape(seqs, length, width))


def solution(mesh):
    in_specs = (
        P(None, "group", None),
        P("group", None, None),
        P(),
        P("group", "mp"),
        P("group", "mp"),
        P("group", "mp"),
        P("group", "mp"),
        P(None, "group", "mp"),
    )
    out_specs = (P(None, "group", "mp"), P(None, "group", None))
    return jax.shard_map(local, mesh=mesh, in_specs=in_specs, out_specs=out_specs, check_vma=False)
```

```python
import functools

import jax
import jax.numpy as jnp
from jax import lax
from jax.experimental import pallas as pl
from jax.experimental.pallas import tpu as pltpu
from jax.sharding import PartitionSpec as P

HEAD_DIM = 128
BF, F32, I32 = jnp.bfloat16, jnp.float32, jnp.int32
PARAMS = pltpu.CompilerParams(vmem_limit_bytes=48 * 1024 * 1024)
NT = (((1,), (1,)), ((), ()))


def iota(shape, dim):
    return lax.broadcasted_iota(I32, shape, dim)


def dot(a, b, dims=(((1,), (0,)), ((), ()))):
    return lax.dot_general(a, b, dims, preferred_element_type=F32)


def bucket_kernel(nchunk, rows_dev, ids_ref, requests_ref, slot_ref):
    seqs, keys = ids_ref.shape
    ids = jnp.concatenate([ids_ref[s : s + 1, :] for s in range(seqs)], axis=1)
    total = seqs * keys
    owner = ids // rows_dev
    lid = ids - owner * rows_dev
    owned = (iota((nchunk, total), 0) == owner).astype(F32)
    owned_bf = owned.astype(BF)
    earlier = (iota((total, total), 0) < iota((total, total), 1)).astype(F32).astype(BF)
    rank = jnp.sum(dot(owned_bf, earlier) * owned, axis=0, keepdims=True).astype(I32)
    placed = iota((128, total), 0) == rank
    high = jnp.where(placed, lid // 32, 0).astype(F32).astype(BF)
    low = jnp.where(placed, lid % 32, 0).astype(F32).astype(BF)
    requests_ref[...] = (dot(owned_bf, high, NT) * 32.0 + dot(owned_bf, low, NT)).astype(I32)
    slot = rank * nchunk + owner
    for s in range(seqs):
        slot_ref[s : s + 1, :] = slot[:, s * keys : (s + 1) * keys]


def fetch_kernel(capacity, asked_ref, table_ref, out_ref):
    nchunk = asked_ref.shape[0]
    rows_dev, feats = table_ref.shape
    asked = pltpu.roll(asked_ref[...], 1, 0)
    lanes = iota((nchunk, rows_dev), 1)
    chosen = jnp.concatenate(
        [(asked[:, s : s + 1] == lanes).astype(F32).astype(BF) for s in range(capacity)], axis=0
    )
    found = dot(chosen, table_ref[...]).astype(BF)
    for s in range(capacity):
        out_ref[:, s * feats : (s + 1) * feats] = found[s * nchunk : (s + 1) * nchunk]


def order_kernel(capacity, slot_ref, rows_ref, one_ref, out_ref):
    seqs, keys = slot_ref.shape
    nchunk = rows_ref.shape[0]
    copies, _, feats = out_ref.shape
    rows = jnp.concatenate(
        [rows_ref[:, s * feats : (s + 1) * feats] for s in range(capacity)], axis=0
    )
    slots = jnp.concatenate([slot_ref[...], jnp.zeros((8 - seqs, keys), I32)], axis=0)
    slots = slots.astype(F32).T.astype(I32)
    lanes = iota((keys, capacity * nchunk), 1)
    for s in range(seqs):
        chosen = (slots[:, s : s + 1] == lanes).astype(F32).astype(BF)
        found = dot(chosen, rows).astype(BF)
        one_ref[s * keys : (s + 1) * keys, :] = found
        for c in range(copies):
            out_ref[c, s * keys : (s + 1) * keys, :] = found


def in_order(weights, run):
    starts = [quad + turn * run for quad in range(0, weights.shape[0], 4 * run) for turn in (0, 2, 1, 3)]
    return jnp.concatenate([weights[start : start + run] for start in starts], axis=0)


def copies_kernel(in_ref, out_ref):
    for c in range(out_ref.shape[0]):
        out_ref[c] = in_ref[...]


def project_kernel(
    run, scal_ref, enc_ref, w_ref, tok_ref, last_tok_ref, q_w_ref, kv_ref, q_ref, kv_acc, q_acc
):
    step, steps = pl.program_id(0), pl.num_programs(0)
    seqs, length, deep = tok_ref.shape

    @pl.when(step == 0)
    def _():
        kv_acc[...] = jnp.zeros_like(kv_acc)
        q_acc[...] = jnp.zeros_like(q_acc)

    is_last = iota((length, deep), 0) == length - 1
    tok = jnp.concatenate(
        [jnp.where(is_last, last_tok_ref[s : s + 1, :], tok_ref[s]) for s in range(seqs)], axis=0
    )
    kv_acc[...] += dot(enc_ref[0], in_order(w_ref[...], run))
    q_acc[...] += dot(tok, in_order(q_w_ref[...], run))

    @pl.when(step == steps - 1)
    def _():
        kv_ref[...] = kv_acc[...]
        q_ref[...] = q_acc[...].astype(BF)


def attend_kernel(
    run, scal_ref, kv_ref, q_ref, enc_ref, w_ref, grad_ref, last_grad_ref, att_ref, dq_ref, kv_acc
):
    step, steps = pl.program_id(0), pl.num_programs(0)
    seqs, length, cols = grad_ref.shape
    keys = kv_acc.shape[0] // seqs

    @pl.when(step == 0)
    def _():
        kv_acc[...] = kv_ref[...]

    kv_acc[...] += dot(enc_ref[0], in_order(w_ref[...], run))

    @pl.when(step == steps - 1)
    def _():
        scale = HEAD_DIM ** (-0.5)
        kv, q = kv_acc[...].astype(BF), q_ref[...]
        last_row = iota((length, HEAD_DIM), 0) == length - 1
        units = [(s, h * HEAD_DIM) for s in range(seqs) for h in range(cols // HEAD_DIM)]
        valid = [last_row | (scal_ref[1 + s] != 0) for s in range(seqs)]
        query = [q[s * length : (s + 1) * length, h : h + HEAD_DIM] for s, h in units]
        key = [kv[s * keys : (s + 1) * keys, h : h + HEAD_DIM] for s, h in units]
        value = [kv[s * keys : (s + 1) * keys, cols + h : cols + h + HEAD_DIM] for s, h in units]
        grad = []
        for s, h in units:
            own = grad_ref[s, :, h : h + HEAD_DIM]
            own = jnp.where(last_row, last_grad_ref[s : s + 1, h : h + HEAD_DIM], own)
            grad.append(jnp.where(valid[s], own, jnp.zeros_like(own)))
        scores = jnp.concatenate([dot(a, b, NT) for a, b in zip(query, key)], axis=0) * scale
        prob_grad = jnp.concatenate([dot(a, b, NT) for a, b in zip(grad, value)], axis=0)
        exps = jnp.exp(scores - jnp.max(scores, axis=-1, keepdims=True))
        prob = exps / jnp.sum(exps, axis=-1, keepdims=True)
        prob_bf = prob.astype(BF)
        mean = jnp.sum(prob * prob_grad, axis=-1, keepdims=True)
        dscore = (prob * (prob_grad - mean) * scale).astype(BF)
        for i, (s, h) in enumerate(units):
            rows = slice(i * length, (i + 1) * length)
            mixed = dot(prob_bf[rows], value[i])
            att_ref[s, :, h : h + HEAD_DIM] = jnp.where(valid[s], mixed, 0.0).astype(BF)
            dq_ref[s, :, h : h + HEAD_DIM] = dot(dscore[rows], key[i]).astype(BF)


def token_kernel(run, att_ref, dq_ref, last_ref, w_ref, att_out, part_ref):
    seqs, length, cols = att_ref.shape
    blocks, _, feats = part_ref.shape
    is_last = iota((length, cols), 0) == length - 1
    rows = jnp.concatenate(
        [jnp.where(is_last, last_ref[s : s + 1, cols:], dq_ref[s]) for s in range(seqs)], axis=0
    )
    for c in range(blocks):
        weights = in_order(w_ref[c * feats : (c + 1) * feats], run)
        part_ref[c] = dot(rows, weights, NT).astype(BF)
    for s in range(seqs):
        att_out[s] = jnp.where(is_last, last_ref[s : s + 1, :cols], att_ref[s])


def sum_kernel(in_ref, out_ref):
    total = in_ref[0].astype(F32)
    for c in range(1, in_ref.shape[0]):
        total = total + in_ref[c].astype(F32)
    rounded = total.astype(BF)
    for c in range(out_ref.shape[0]):
        out_ref[c] = rounded


def join_kernel(in_ref, out_ref):
    feats = in_ref.shape[2]
    for c in range(in_ref.shape[0]):
        out_ref[:, c * feats : (c + 1) * feats] = in_ref[c]


def after(value, *earlier):
    return lax.optimization_barrier((value, earlier))[0]


def local(
    tokens, neighbour_ids, group_document, embed_table, w_query, w_key, w_value, attended_grad
):
    nchunk = lax.axis_size("group")
    mp_size = lax.axis_size("mp")
    group_here = lax.axis_index("group")
    seqs, length, width = tokens.shape
    run, cols = w_query.shape
    keys = neighbour_ids.shape[2]
    id_count = seqs * keys
    rows_dev, feats = embed_table.shape
    capacity = max(2, 3 * id_count // (2 * nchunk))
    onward = [(g, (g + 1) % nchunk) for g in range(nchunk)]
    backward = [(g, (g - 1) % nchunk) for g in range(nchunk)]

    def paired(own, near):
        lower = (group_here // 2) % 2 == 0
        return jnp.concatenate([jnp.where(lower, own, near), jnp.where(lower, near, own)], axis=0)

    def round_z(value):
        groups = [
            [z * 4 + y * 2 + c for z in range(nchunk // 4) for c in range(2)] for y in range(2)
        ]
        return lax.all_gather(value, "group", axis=0, tiled=True, axis_index_groups=groups)

    own = jnp.concatenate([w_key, w_value, w_query], axis=1)
    pair = paired(own, lax.ppermute(own, "group", [(g, g ^ 2) for g in range(nchunk)]))

    last_row = lax.ppermute(
        jnp.concatenate([tokens[:, -1], attended_grad[:, -1]], axis=1), "group", onward
    )

    requests, slot = pl.pallas_call(
        functools.partial(bucket_kernel, nchunk, rows_dev),
        out_shape=[
            jax.ShapeDtypeStruct((nchunk, 128), I32),
            jax.ShapeDtypeStruct((seqs, keys), I32),
        ],
        compiler_params=PARAMS,
    )(neighbour_ids.reshape(seqs, keys))
    slot = lax.ppermute(slot, "group", onward)
    asked = lax.all_to_all(requests, "group", split_axis=0, concat_axis=0, tiled=True)
    weights = round_z(after(pair, asked))
    found = pl.pallas_call(
        functools.partial(fetch_kernel, capacity),
        out_shape=jax.ShapeDtypeStruct((nchunk, capacity * feats), BF),
        compiler_params=PARAMS,
    )(asked, embed_table)
    found = found.reshape(nchunk, 2, -1)
    returned = lax.all_to_all(found, "group", split_axis=0, concat_axis=0, tiled=True)
    returned = after(returned.reshape(nchunk, -1), last_row)
    across_x = mp_size // 2
    along_x = [[2 * x + y for x in range(across_x)] for y in range(2)]
    copies = jax.ShapeDtypeStruct((across_x, id_count, feats), BF)

    def round_x(value):
        return lax.all_to_all(
            value, "mp", split_axis=0, concat_axis=0, tiled=True, axis_index_groups=along_x
        )

    single, encoded = pl.pallas_call(
        functools.partial(order_kernel, capacity),
        out_shape=[jax.ShapeDtypeStruct((id_count, feats), BF), copies],
        compiler_params=PARAMS,
    )(slot, returned)
    single = lax.ppermute(single, "mp", [(m, m ^ 1) for m in range(mp_size)])
    encoded = round_x(encoded)
    encoded_other = round_x(
        pl.pallas_call(copies_kernel, out_shape=copies, compiler_params=PARAMS)(single)
    )

    earlier = jnp.maximum(group_here - 1, 0)
    doc_here = lax.dynamic_slice_in_dim(group_document, group_here, 1, 1)[:, 0]
    doc_before = lax.dynamic_slice_in_dim(group_document, earlier, 1, 1)[:, 0]
    same_doc = (group_here >= 1) & (doc_here == doc_before)
    y_hi = lax.axis_index("mp") % 2
    scalars = jnp.concatenate([y_hi[None].astype(I32), same_doc.astype(I32)])
    whole = lambda *shape: pl.BlockSpec(shape, lambda i, s: (0,) * len(shape))
    kv_part, query = pl.pallas_call(
        functools.partial(project_kernel, run),
        grid_spec=pltpu.PrefetchScalarGridSpec(
            num_scalar_prefetch=1,
            grid=(across_x,),
            in_specs=[
                pl.BlockSpec((1, id_count, feats), lambda i, s: (i, 0, 0)),
                pl.BlockSpec((feats, 2 * cols), lambda i, s: (2 * i + s[0], 0)),
                pl.BlockSpec((seqs, length, 2 * feats), lambda i, s: (0, 0, i)),
                pl.BlockSpec((seqs, 2 * feats), lambda i, s: (0, i)),
                pl.BlockSpec((2 * feats, cols), lambda i, s: (i, 2)),
            ],
            out_specs=[whole(id_count, 2 * cols), whole(seqs * length, cols)],
            scratch_shapes=[
                pltpu.VMEM((id_count, 2 * cols), F32),
                pltpu.VMEM((seqs * length, cols), F32),
            ],
        ),
        out_shape=[
            jax.ShapeDtypeStruct((id_count, 2 * cols), F32),
            jax.ShapeDtypeStruct((seqs * length, cols), BF),
        ],
        compiler_params=PARAMS,
    )(scalars, encoded, weights, tokens, last_row, weights)
    att, dquery = pl.pallas_call(
        functools.partial(attend_kernel, run),
        grid_spec=pltpu.PrefetchScalarGridSpec(
            num_scalar_prefetch=1,
            grid=(across_x,),
            in_specs=[
                whole(id_count, 2 * cols),
                whole(seqs * length, cols),
                pl.BlockSpec((1, id_count, feats), lambda i, s: (i, 0, 0)),
                pl.BlockSpec((feats, 2 * cols), lambda i, s: (2 * i + 1 - s[0], 0)),
                whole(seqs, length, cols),
                pl.BlockSpec((seqs, cols), lambda i, s: (0, width // cols)),
            ],
            out_specs=[whole(seqs, length, cols), whole(seqs, length, cols)],
            scratch_shapes=[pltpu.VMEM((id_count, 2 * cols), F32)],
        ),
        out_shape=[jax.ShapeDtypeStruct((seqs, length, cols), BF)] * 2,
        compiler_params=PARAMS,
    )(scalars, kv_part, query, encoded_other, weights, attended_grad, last_row)

    last = lax.ppermute(
        jnp.concatenate([att[:, -1], dquery[:, -1]], axis=-1), "group", backward
    )
    fixed = lambda *shape: pl.BlockSpec(shape, lambda i: (0,) * len(shape))
    attended, part = pl.pallas_call(
        functools.partial(token_kernel, run),
        grid=(1,),
        in_specs=[
            fixed(seqs, length, cols),
            fixed(seqs, length, cols),
            fixed(seqs, 2 * cols),
            pl.BlockSpec((width, cols), lambda i: (0, 2)),
        ],
        out_specs=[fixed(seqs, length, cols), fixed(mp_size, seqs * length, feats)],
        out_shape=[
            jax.ShapeDtypeStruct((seqs, length, cols), BF),
            jax.ShapeDtypeStruct((mp_size, seqs * length, feats), BF),
        ],
        compiler_params=PARAMS,
    )(att, dquery, last, weights)
    part = lax.all_to_all(part, "mp", split_axis=0, concat_axis=0, tiled=True)
    part = pl.pallas_call(
        sum_kernel,
        out_shape=jax.ShapeDtypeStruct((mp_size, seqs * length, feats), BF),
        compiler_params=PARAMS,
    )(part)
    part = lax.all_to_all(part, "mp", split_axis=0, concat_axis=0, tiled=True)
    token_grad = pl.pallas_call(
        join_kernel,
        grid=(mp_size // 2,),
        in_specs=[pl.BlockSpec((2, seqs * length, feats), lambda i: (i, 0, 0))],
        out_specs=pl.BlockSpec((seqs * length, 2 * feats), lambda i: (0, i)),
        out_shape=jax.ShapeDtypeStruct((seqs * length, width), BF),
        compiler_params=PARAMS,
    )(part)
    return (attended, token_grad.reshape(seqs, length, width))


def solution(mesh):
    in_specs = (
        P(None, "group", None),
        P("group", None, None),
        P(),
        P("group", "mp"),
        P("group", "mp"),
        P("group", "mp"),
        P("group", "mp"),
        P(None, "group", "mp"),
    )
    out_specs = (P(None, "group", "mp"), P(None, "group", None))
    return jax.shard_map(local, mesh=mesh, in_specs=in_specs, out_specs=out_specs, check_vma=False)
```

```python
import functools

import jax
import jax.numpy as jnp
from jax import lax
from jax.experimental import pallas as pl
from jax.experimental.pallas import tpu as pltpu
from jax.sharding import PartitionSpec as P

HEAD_DIM = 128
BF, F32, I32 = jnp.bfloat16, jnp.float32, jnp.int32
PARAMS = pltpu.CompilerParams(vmem_limit_bytes=48 * 1024 * 1024)
NT = (((1,), (1,)), ((), ()))


def iota(shape, dim):
    return lax.broadcasted_iota(I32, shape, dim)


def dot(a, b, dims=(((1,), (0,)), ((), ()))):
    return lax.dot_general(a, b, dims, preferred_element_type=F32)


def bucket_kernel(nchunk, rows_dev, ids_ref, requests_ref, slot_ref):
    seqs, keys = ids_ref.shape
    ids = jnp.concatenate([ids_ref[s : s + 1, :] for s in range(seqs)], axis=1)
    total = seqs * keys
    owner = ids // rows_dev
    lid = ids - owner * rows_dev
    owned = (iota((nchunk, total), 0) == owner).astype(F32)
    owned_bf = owned.astype(BF)
    earlier = (iota((total, total), 0) < iota((total, total), 1)).astype(F32).astype(BF)
    rank = jnp.sum(dot(owned_bf, earlier) * owned, axis=0, keepdims=True).astype(I32)
    placed = iota((128, total), 0) == rank
    high = jnp.where(placed, lid // 32, 0).astype(F32).astype(BF)
    low = jnp.where(placed, lid % 32, 0).astype(F32).astype(BF)
    requests_ref[...] = (dot(owned_bf, high, NT) * 32.0 + dot(owned_bf, low, NT)).astype(I32)
    slot = rank * nchunk + owner
    for s in range(seqs):
        slot_ref[s : s + 1, :] = slot[:, s * keys : (s + 1) * keys]


def fetch_kernel(capacity, asked_ref, table_ref, out_ref):
    nchunk = asked_ref.shape[0]
    rows_dev, feats = table_ref.shape
    asked = pltpu.roll(asked_ref[...], 1, 0)
    lanes = iota((nchunk, rows_dev), 1)
    chosen = jnp.concatenate(
        [(asked[:, s : s + 1] == lanes).astype(F32).astype(BF) for s in range(capacity)], axis=0
    )
    found = dot(chosen, table_ref[...]).astype(BF)
    for s in range(capacity):
        out_ref[:, s * feats : (s + 1) * feats] = found[s * nchunk : (s + 1) * nchunk]


def order_kernel(capacity, slot_ref, rows_ref, one_ref, out_ref):
    seqs, keys = slot_ref.shape
    nchunk = rows_ref.shape[0]
    copies, _, feats = out_ref.shape
    rows = jnp.concatenate(
        [rows_ref[:, s * feats : (s + 1) * feats] for s in range(capacity)], axis=0
    )
    slots = jnp.concatenate([slot_ref[...], jnp.zeros((8 - seqs, keys), I32)], axis=0)
    slots = slots.astype(F32).T.astype(I32)
    lanes = iota((keys, capacity * nchunk), 1)
    for s in range(seqs):
        chosen = (slots[:, s : s + 1] == lanes).astype(F32).astype(BF)
        found = dot(chosen, rows).astype(BF)
        one_ref[s * keys : (s + 1) * keys, :] = found
        for c in range(copies):
            out_ref[c, s * keys : (s + 1) * keys, :] = found


def in_order(weights, run):
    starts = [quad + turn * run for quad in range(0, weights.shape[0], 4 * run) for turn in (0, 2, 1, 3)]
    return jnp.concatenate([weights[start : start + run] for start in starts], axis=0)


def copies_kernel(in_ref, out_ref):
    for c in range(out_ref.shape[0]):
        out_ref[c] = in_ref[...]


def project_kernel(
    run, scal_ref, enc_ref, w_ref, next_w_ref, tok_ref, last_tok_ref, q_w_ref, kv_ref, q_ref, kv_acc,
    q_acc,
):
    step, steps = pl.program_id(0), pl.num_programs(0)
    seqs, length, deep = tok_ref.shape

    @pl.when(step == 0)
    def _():
        kv_acc[...] = jnp.zeros_like(kv_acc)
        q_acc[...] = jnp.zeros_like(q_acc)

    is_last = iota((length, deep), 0) == length - 1
    tok = jnp.concatenate(
        [jnp.where(is_last, last_tok_ref[s : s + 1, :], tok_ref[s]) for s in range(seqs)], axis=0
    )
    enc = jnp.concatenate([enc_ref[0], enc_ref[1]], axis=1)
    weights = jnp.concatenate([in_order(w_ref[...], run), in_order(next_w_ref[...], run)], axis=0)
    kv_acc[...] += dot(enc, weights)
    q_acc[...] += dot(tok, in_order(q_w_ref[...], run))

    @pl.when(step == steps - 1)
    def _():
        kv_ref[...] = kv_acc[...]
        q_ref[...] = q_acc[...].astype(BF)


def attend_kernel(
    run, scal_ref, kv_ref, q_ref, enc_ref, w_ref, next_w_ref, grad_ref, last_grad_ref, att_ref, dq_ref,
    kv_acc,
):
    step, steps = pl.program_id(0), pl.num_programs(0)
    seqs, length, cols = grad_ref.shape
    keys = kv_acc.shape[0] // seqs

    @pl.when(step == 0)
    def _():
        kv_acc[...] = kv_ref[...]

    enc = jnp.concatenate([enc_ref[0], enc_ref[1]], axis=1)
    weights = jnp.concatenate([in_order(w_ref[...], run), in_order(next_w_ref[...], run)], axis=0)
    kv_acc[...] += dot(enc, weights)

    @pl.when(step == steps - 1)
    def _():
        scale = HEAD_DIM ** (-0.5)
        kv, q = kv_acc[...].astype(BF), q_ref[...]
        last_row = iota((length, HEAD_DIM), 0) == length - 1
        units = [(s, h * HEAD_DIM) for s in range(seqs) for h in range(cols // HEAD_DIM)]
        valid = [last_row | (scal_ref[1 + s] != 0) for s in range(seqs)]
        query = [q[s * length : (s + 1) * length, h : h + HEAD_DIM] for s, h in units]
        key = [kv[s * keys : (s + 1) * keys, h : h + HEAD_DIM] for s, h in units]
        value = [kv[s * keys : (s + 1) * keys, cols + h : cols + h + HEAD_DIM] for s, h in units]
        grad = []
        for s, h in units:
            own = grad_ref[s, :, h : h + HEAD_DIM]
            own = jnp.where(last_row, last_grad_ref[s : s + 1, h : h + HEAD_DIM], own)
            grad.append(jnp.where(valid[s], own, jnp.zeros_like(own)))
        scores = jnp.concatenate([dot(a, b, NT) for a, b in zip(query, key)], axis=0) * scale
        prob_grad = jnp.concatenate([dot(a, b, NT) for a, b in zip(grad, value)], axis=0)
        exps = jnp.exp(scores - jnp.max(scores, axis=-1, keepdims=True))
        prob = exps / jnp.sum(exps, axis=-1, keepdims=True)
        prob_bf = prob.astype(BF)
        mean = jnp.sum(prob * prob_grad, axis=-1, keepdims=True)
        dscore = (prob * (prob_grad - mean) * scale).astype(BF)
        for i, (s, h) in enumerate(units):
            rows = slice(i * length, (i + 1) * length)
            mixed = dot(prob_bf[rows], value[i])
            att_ref[s, :, h : h + HEAD_DIM] = jnp.where(valid[s], mixed, 0.0).astype(BF)
            dq_ref[s, :, h : h + HEAD_DIM] = dot(dscore[rows], key[i]).astype(BF)


def token_kernel(run, att_ref, dq_ref, last_ref, w_ref, att_out, part_ref):
    seqs, length, cols = att_ref.shape
    blocks, _, feats = part_ref.shape
    is_last = iota((length, cols), 0) == length - 1
    rows = jnp.concatenate(
        [jnp.where(is_last, last_ref[s : s + 1, cols:], dq_ref[s]) for s in range(seqs)], axis=0
    )
    for c in range(blocks):
        weights = in_order(w_ref[c * feats : (c + 1) * feats], run)
        part_ref[c] = dot(rows, weights, NT).astype(BF)
    for s in range(seqs):
        att_out[s] = jnp.where(is_last, last_ref[s : s + 1, :cols], att_ref[s])


def sum_kernel(in_ref, out_ref):
    total = in_ref[0].astype(F32)
    for c in range(1, in_ref.shape[0]):
        total = total + in_ref[c].astype(F32)
    rounded = total.astype(BF)
    for c in range(out_ref.shape[0]):
        out_ref[c] = rounded


def join_kernel(in_ref, out_ref):
    feats = in_ref.shape[2]
    for c in range(in_ref.shape[0]):
        out_ref[:, c * feats : (c + 1) * feats] = in_ref[c]


def after(value, *earlier):
    return lax.optimization_barrier((value, earlier))[0]


def local(
    tokens, neighbour_ids, group_document, embed_table, w_query, w_key, w_value, attended_grad
):
    nchunk = lax.axis_size("group")
    mp_size = lax.axis_size("mp")
    group_here = lax.axis_index("group")
    seqs, length, width = tokens.shape
    run, cols = w_query.shape
    keys = neighbour_ids.shape[2]
    id_count = seqs * keys
    rows_dev, feats = embed_table.shape
    capacity = max(2, 3 * id_count // (2 * nchunk))
    onward = [(g, (g + 1) % nchunk) for g in range(nchunk)]
    backward = [(g, (g - 1) % nchunk) for g in range(nchunk)]

    def paired(own, near):
        lower = (group_here // 2) % 2 == 0
        return jnp.concatenate([jnp.where(lower, own, near), jnp.where(lower, near, own)], axis=0)

    def round_z(value):
        groups = [
            [z * 4 + y * 2 + c for z in range(nchunk // 4) for c in range(2)] for y in range(2)
        ]
        return lax.all_gather(value, "group", axis=0, tiled=True, axis_index_groups=groups)

    zero = jnp.zeros((), BF)
    own = sum(
        lax.pad(block, zero, ((0, 0, 0), (i * cols, (2 - i) * cols, 0)))
        for i, block in enumerate((w_key, w_value, w_query))
    )
    pair = paired(own, lax.ppermute(own, "group", [(g, g ^ 2) for g in range(nchunk)]))

    last_row = lax.ppermute(
        jnp.concatenate([tokens[:, -1], attended_grad[:, -1]], axis=1), "group", onward
    )

    requests, slot = pl.pallas_call(
        functools.partial(bucket_kernel, nchunk, rows_dev),
        out_shape=[
            jax.ShapeDtypeStruct((nchunk, 128), I32),
            jax.ShapeDtypeStruct((seqs, keys), I32),
        ],
        compiler_params=PARAMS,
    )(neighbour_ids.reshape(seqs, keys))
    slot = lax.ppermute(slot, "group", onward)
    asked = lax.all_to_all(requests, "group", split_axis=0, concat_axis=0, tiled=True)
    weights = round_z(after(pair, asked))
    found = pl.pallas_call(
        functools.partial(fetch_kernel, capacity),
        out_shape=jax.ShapeDtypeStruct((nchunk, capacity * feats), BF),
        compiler_params=PARAMS,
    )(asked, embed_table)
    found = found.reshape(nchunk, 2, -1)
    returned = lax.all_to_all(found, "group", split_axis=0, concat_axis=0, tiled=True)
    returned = after(returned.reshape(nchunk, -1), last_row)
    across_x = mp_size // 2
    along_x = [[2 * x + y for x in range(across_x)] for y in range(2)]
    copies = jax.ShapeDtypeStruct((across_x, id_count, feats), BF)

    def round_x(value):
        return lax.all_to_all(
            value, "mp", split_axis=0, concat_axis=0, tiled=True, axis_index_groups=along_x
        )

    single, encoded = pl.pallas_call(
        functools.partial(order_kernel, capacity),
        out_shape=[jax.ShapeDtypeStruct((id_count, feats), BF), copies],
        compiler_params=PARAMS,
    )(slot, returned)
    single = lax.ppermute(single, "mp", [(m, m ^ 1) for m in range(mp_size)])
    encoded = round_x(encoded)
    encoded_other = round_x(
        pl.pallas_call(copies_kernel, out_shape=copies, compiler_params=PARAMS)(single)
    )

    earlier = jnp.maximum(group_here - 1, 0)
    doc_here = lax.dynamic_slice_in_dim(group_document, group_here, 1, 1)[:, 0]
    doc_before = lax.dynamic_slice_in_dim(group_document, earlier, 1, 1)[:, 0]
    same_doc = (group_here >= 1) & (doc_here == doc_before)
    y_hi = lax.axis_index("mp") % 2
    scalars = jnp.concatenate([y_hi[None].astype(I32), same_doc.astype(I32)])
    whole = lambda *shape: pl.BlockSpec(shape, lambda i, s: (0,) * len(shape))
    kv_part, query = pl.pallas_call(
        functools.partial(project_kernel, run),
        grid_spec=pltpu.PrefetchScalarGridSpec(
            num_scalar_prefetch=1,
            grid=(across_x // 2,),
            in_specs=[
                pl.BlockSpec((2, id_count, feats), lambda i, s: (i, 0, 0)),
                pl.BlockSpec((feats, 2 * cols), lambda i, s: (4 * i + s[0], 0)),
                pl.BlockSpec((feats, 2 * cols), lambda i, s: (4 * i + 2 + s[0], 0)),
                pl.BlockSpec((seqs, length, 4 * feats), lambda i, s: (0, 0, i)),
                pl.BlockSpec((seqs, 4 * feats), lambda i, s: (0, i)),
                pl.BlockSpec((4 * feats, cols), lambda i, s: (i, 2)),
            ],
            out_specs=[whole(id_count, 2 * cols), whole(seqs * length, cols)],
            scratch_shapes=[
                pltpu.VMEM((id_count, 2 * cols), F32),
                pltpu.VMEM((seqs * length, cols), F32),
            ],
        ),
        out_shape=[
            jax.ShapeDtypeStruct((id_count, 2 * cols), F32),
            jax.ShapeDtypeStruct((seqs * length, cols), BF),
        ],
        compiler_params=PARAMS,
    )(scalars, encoded, weights, weights, tokens, last_row, weights)
    att, dquery = pl.pallas_call(
        functools.partial(attend_kernel, run),
        grid_spec=pltpu.PrefetchScalarGridSpec(
            num_scalar_prefetch=1,
            grid=(across_x // 2,),
            in_specs=[
                whole(id_count, 2 * cols),
                whole(seqs * length, cols),
                pl.BlockSpec((2, id_count, feats), lambda i, s: (i, 0, 0)),
                pl.BlockSpec((feats, 2 * cols), lambda i, s: (4 * i + 1 - s[0], 0)),
                pl.BlockSpec((feats, 2 * cols), lambda i, s: (4 * i + 3 - s[0], 0)),
                whole(seqs, length, cols),
                pl.BlockSpec((seqs, cols), lambda i, s: (0, width // cols)),
            ],
            out_specs=[whole(seqs, length, cols), whole(seqs, length, cols)],
            scratch_shapes=[pltpu.VMEM((id_count, 2 * cols), F32)],
        ),
        out_shape=[jax.ShapeDtypeStruct((seqs, length, cols), BF)] * 2,
        compiler_params=PARAMS,
    )(scalars, kv_part, query, encoded_other, weights, weights, attended_grad, last_row)

    last = lax.ppermute(
        jnp.concatenate([att[:, -1], dquery[:, -1]], axis=-1), "group", backward
    )
    fixed = lambda *shape: pl.BlockSpec(shape, lambda i: (0,) * len(shape))
    attended, part = pl.pallas_call(
        functools.partial(token_kernel, run),
        grid=(1,),
        in_specs=[
            fixed(seqs, length, cols),
            fixed(seqs, length, cols),
            fixed(seqs, 2 * cols),
            pl.BlockSpec((width, cols), lambda i: (0, 2)),
        ],
        out_specs=[fixed(seqs, length, cols), fixed(mp_size, seqs * length, feats)],
        out_shape=[
            jax.ShapeDtypeStruct((seqs, length, cols), BF),
            jax.ShapeDtypeStruct((mp_size, seqs * length, feats), BF),
        ],
        compiler_params=PARAMS,
    )(att, dquery, last, weights)
    part = lax.all_to_all(part, "mp", split_axis=0, concat_axis=0, tiled=True)
    part = pl.pallas_call(
        sum_kernel,
        out_shape=jax.ShapeDtypeStruct((mp_size, seqs * length, feats), BF),
        compiler_params=PARAMS,
    )(part)
    part = lax.all_to_all(part, "mp", split_axis=0, concat_axis=0, tiled=True)
    token_grad = pl.pallas_call(
        join_kernel,
        grid=(mp_size // 2,),
        in_specs=[pl.BlockSpec((2, seqs * length, feats), lambda i: (i, 0, 0))],
        out_specs=pl.BlockSpec((seqs * length, 2 * feats), lambda i: (0, i)),
        out_shape=jax.ShapeDtypeStruct((seqs * length, width), BF),
        compiler_params=PARAMS,
    )(part)
    return (attended, token_grad.reshape(seqs, length, width))


def solution(mesh):
    in_specs = (
        P(None, "group", None),
        P("group", None, None),
        P(),
        P("group", "mp"),
        P("group", "mp"),
        P("group", "mp"),
        P("group", "mp"),
        P(None, "group", "mp"),
    )
    out_specs = (P(None, "group", "mp"), P(None, "group", None))
    return jax.shard_map(local, mesh=mesh, in_specs=in_specs, out_specs=out_specs, check_vma=False)
```

```python
import functools

import jax
import jax.numpy as jnp
from jax import lax
from jax.experimental import pallas as pl
from jax.experimental.pallas import tpu as pltpu
from jax.sharding import PartitionSpec as P

HEAD_DIM = 128
BF, F32, I32 = jnp.bfloat16, jnp.float32, jnp.int32
PARAMS = pltpu.CompilerParams(vmem_limit_bytes=48 * 1024 * 1024)
NT = (((1,), (1,)), ((), ()))


def iota(shape, dim):
    return lax.broadcasted_iota(I32, shape, dim)


def dot(a, b, dims=(((1,), (0,)), ((), ()))):
    return lax.dot_general(a, b, dims, preferred_element_type=F32)


def bucket_kernel(nchunk, rows_dev, ids_ref, requests_ref, slot_ref):
    seqs, keys = ids_ref.shape
    ids = jnp.concatenate([ids_ref[s : s + 1, :] for s in range(seqs)], axis=1)
    total = seqs * keys
    owner = ids // rows_dev
    lid = ids - owner * rows_dev
    owned = (iota((nchunk, total), 0) == owner).astype(F32)
    owned_bf = owned.astype(BF)
    earlier = (iota((total, total), 0) < iota((total, total), 1)).astype(F32).astype(BF)
    rank = jnp.sum(dot(owned_bf, earlier) * owned, axis=0, keepdims=True).astype(I32)
    placed = iota((128, total), 0) == rank
    high = jnp.where(placed, lid // 32, 0).astype(F32).astype(BF)
    low = jnp.where(placed, lid % 32, 0).astype(F32).astype(BF)
    requests_ref[...] = (dot(owned_bf, high, NT) * 32.0 + dot(owned_bf, low, NT)).astype(I32)
    slot = rank * nchunk + owner
    for s in range(seqs):
        slot_ref[s : s + 1, :] = slot[:, s * keys : (s + 1) * keys]


def fetch_kernel(capacity, asked_ref, table_ref, out_ref):
    nchunk = asked_ref.shape[0]
    rows_dev, feats = table_ref.shape
    asked = pltpu.roll(asked_ref[...], 1, 0)
    lanes = iota((nchunk, rows_dev), 1)
    chosen = jnp.concatenate(
        [(asked[:, s : s + 1] == lanes).astype(F32).astype(BF) for s in range(capacity)], axis=0
    )
    found = dot(chosen, table_ref[...]).astype(BF)
    for s in range(capacity):
        out_ref[:, s * feats : (s + 1) * feats] = found[s * nchunk : (s + 1) * nchunk]


def order_kernel(capacity, slot_ref, rows_ref, one_ref, out_ref):
    seqs, keys = slot_ref.shape
    nchunk = rows_ref.shape[0]
    copies, _, feats = out_ref.shape
    rows = jnp.concatenate(
        [rows_ref[:, s * feats : (s + 1) * feats] for s in range(capacity)], axis=0
    )
    slots = jnp.concatenate([slot_ref[...], jnp.zeros((8 - seqs, keys), I32)], axis=0)
    slots = slots.astype(F32).T.astype(I32)
    lanes = iota((keys, capacity * nchunk), 1)
    for s in range(seqs):
        chosen = (slots[:, s : s + 1] == lanes).astype(F32).astype(BF)
        found = dot(chosen, rows).astype(BF)
        one_ref[s * keys : (s + 1) * keys, :] = found
        for c in range(copies):
            out_ref[c, s * keys : (s + 1) * keys, :] = found


def in_order(weights, run):
    starts = [quad + turn * run for quad in range(0, weights.shape[0], 4 * run) for turn in (0, 2, 1, 3)]
    return jnp.concatenate([weights[start : start + run] for start in starts], axis=0)


def copies_kernel(in_ref, out_ref):
    for c in range(out_ref.shape[0]):
        out_ref[c] = in_ref[...]


def project_kernel(run, tok_ref, last_tok_ref, q_w_ref, q_ref, q_acc):
    step, steps = pl.program_id(0), pl.num_programs(0)
    seqs, length, deep = tok_ref.shape

    @pl.when(step == 0)
    def _():
        q_acc[...] = jnp.zeros_like(q_acc)

    is_last = iota((length, deep), 0) == length - 1
    tok = jnp.concatenate(
        [jnp.where(is_last, last_tok_ref[s : s + 1, :], tok_ref[s]) for s in range(seqs)], axis=0
    )
    q_acc[...] += dot(tok, in_order(q_w_ref[...], run))

    @pl.when(step == steps - 1)
    def _():
        q_ref[...] = q_acc[...].astype(BF)


def attend_kernel(
    run, scal_ref, q_ref, enc_ref, other_ref, w_ref, next_w_ref, grad_ref, last_grad_ref, att_ref, dq_ref,
    kv_acc,
):
    step, steps = pl.program_id(0), pl.num_programs(0)
    seqs, length, cols = grad_ref.shape
    keys = kv_acc.shape[0] // seqs

    @pl.when(step == 0)
    def _():
        kv_acc[...] = jnp.zeros_like(kv_acc)

    def add(ref):
        enc = jnp.concatenate([ref[0], ref[1]], axis=1)
        weights = jnp.concatenate([in_order(w_ref[...], run), in_order(next_w_ref[...], run)], axis=0)
        kv_acc[...] += dot(enc, weights)

    @pl.when(step < steps // 2)
    def _():
        add(enc_ref)

    @pl.when(step >= steps // 2)
    def _():
        add(other_ref)

    @pl.when(step == steps - 1)
    def _():
        scale = HEAD_DIM ** (-0.5)
        kv, q = kv_acc[...].astype(BF), q_ref[...]
        last_row = iota((length, HEAD_DIM), 0) == length - 1
        units = [(s, h * HEAD_DIM) for s in range(seqs) for h in range(cols // HEAD_DIM)]
        valid = [last_row | (scal_ref[1 + s] != 0) for s in range(seqs)]
        query = [q[s * length : (s + 1) * length, h : h + HEAD_DIM] for s, h in units]
        key = [kv[s * keys : (s + 1) * keys, h : h + HEAD_DIM] for s, h in units]
        value = [kv[s * keys : (s + 1) * keys, cols + h : cols + h + HEAD_DIM] for s, h in units]
        grad = []
        for s, h in units:
            own = grad_ref[s, :, h : h + HEAD_DIM]
            own = jnp.where(last_row, last_grad_ref[s : s + 1, h : h + HEAD_DIM], own)
            grad.append(jnp.where(valid[s], own, jnp.zeros_like(own)))
        scores = jnp.concatenate([dot(a, b, NT) for a, b in zip(query, key)], axis=0) * scale
        prob_grad = jnp.concatenate([dot(a, b, NT) for a, b in zip(grad, value)], axis=0)
        exps = jnp.exp(scores - jnp.max(scores, axis=-1, keepdims=True))
        prob = exps / jnp.sum(exps, axis=-1, keepdims=True)
        prob_bf = prob.astype(BF)
        mean = jnp.sum(prob * prob_grad, axis=-1, keepdims=True)
        dscore = (prob * (prob_grad - mean) * scale).astype(BF)
        for i, (s, h) in enumerate(units):
            rows = slice(i * length, (i + 1) * length)
            mixed = dot(prob_bf[rows], value[i])
            att_ref[s, :, h : h + HEAD_DIM] = jnp.where(valid[s], mixed, 0.0).astype(BF)
            dq_ref[s, :, h : h + HEAD_DIM] = dot(dscore[rows], key[i]).astype(BF)


def token_kernel(run, att_ref, dq_ref, last_ref, w_ref, att_out, part_ref):
    seqs, length, cols = att_ref.shape
    blocks, _, feats = part_ref.shape
    is_last = iota((length, cols), 0) == length - 1
    rows = jnp.concatenate(
        [jnp.where(is_last, last_ref[s : s + 1, cols:], dq_ref[s]) for s in range(seqs)], axis=0
    )
    for c in range(blocks):
        weights = in_order(w_ref[c * feats : (c + 1) * feats], run)
        part_ref[c] = dot(rows, weights, NT).astype(BF)
    for s in range(seqs):
        att_out[s] = jnp.where(is_last, last_ref[s : s + 1, :cols], att_ref[s])


def sum_kernel(in_ref, out_ref):
    total = in_ref[0].astype(F32)
    for c in range(1, in_ref.shape[0]):
        total = total + in_ref[c].astype(F32)
    rounded = total.astype(BF)
    for c in range(out_ref.shape[0]):
        out_ref[c] = rounded


def join_kernel(in_ref, out_ref):
    feats = in_ref.shape[2]
    for c in range(in_ref.shape[0]):
        out_ref[:, c * feats : (c + 1) * feats] = in_ref[c]


def after(value, *earlier):
    return lax.optimization_barrier((value, earlier))[0]


def local(
    tokens, neighbour_ids, group_document, embed_table, w_query, w_key, w_value, attended_grad
):
    nchunk = lax.axis_size("group")
    mp_size = lax.axis_size("mp")
    group_here = lax.axis_index("group")
    seqs, length, width = tokens.shape
    run, cols = w_query.shape
    keys = neighbour_ids.shape[2]
    id_count = seqs * keys
    rows_dev, feats = embed_table.shape
    capacity = max(2, 3 * id_count // (2 * nchunk))
    onward = [(g, (g + 1) % nchunk) for g in range(nchunk)]
    backward = [(g, (g - 1) % nchunk) for g in range(nchunk)]

    def paired(own, near):
        lower = (group_here // 2) % 2 == 0
        return jnp.concatenate([jnp.where(lower, own, near), jnp.where(lower, near, own)], axis=0)

    def round_z(value):
        groups = [
            [z * 4 + y * 2 + c for z in range(nchunk // 4) for c in range(2)] for y in range(2)
        ]
        return lax.all_gather(value, "group", axis=0, tiled=True, axis_index_groups=groups)

    zero = jnp.zeros((), BF)
    own = sum(
        lax.pad(block, zero, ((0, 0, 0), (i * cols, (2 - i) * cols, 0)))
        for i, block in enumerate((w_key, w_value, w_query))
    )
    pair = paired(own, lax.ppermute(own, "group", [(g, g ^ 2) for g in range(nchunk)]))

    last_row = lax.ppermute(
        jnp.concatenate([tokens[:, -1], attended_grad[:, -1]], axis=1), "group", onward
    )

    requests, slot = pl.pallas_call(
        functools.partial(bucket_kernel, nchunk, rows_dev),
        out_shape=[
            jax.ShapeDtypeStruct((nchunk, 128), I32),
            jax.ShapeDtypeStruct((seqs, keys), I32),
        ],
        compiler_params=PARAMS,
    )(neighbour_ids.reshape(seqs, keys))
    slot = lax.ppermute(slot, "group", onward)
    asked = lax.all_to_all(requests, "group", split_axis=0, concat_axis=0, tiled=True)
    weights = round_z(after(pair, asked))
    found = pl.pallas_call(
        functools.partial(fetch_kernel, capacity),
        out_shape=jax.ShapeDtypeStruct((nchunk, capacity * feats), BF),
        compiler_params=PARAMS,
    )(asked, embed_table)
    found = found.reshape(nchunk, 2, -1)
    returned = lax.all_to_all(found, "group", split_axis=0, concat_axis=0, tiled=True)
    returned = after(returned.reshape(nchunk, -1), last_row)
    across_x = mp_size // 2
    along_x = [[2 * x + y for x in range(across_x)] for y in range(2)]
    copies = jax.ShapeDtypeStruct((across_x, id_count, feats), BF)

    def round_x(value):
        return lax.all_to_all(
            value, "mp", split_axis=0, concat_axis=0, tiled=True, axis_index_groups=along_x
        )

    single, encoded = pl.pallas_call(
        functools.partial(order_kernel, capacity),
        out_shape=[jax.ShapeDtypeStruct((id_count, feats), BF), copies],
        compiler_params=PARAMS,
    )(slot, returned)
    single = lax.ppermute(single, "mp", [(m, m ^ 1) for m in range(mp_size)])
    encoded = round_x(encoded)
    encoded_other = round_x(
        pl.pallas_call(copies_kernel, out_shape=copies, compiler_params=PARAMS)(single)
    )

    earlier = jnp.maximum(group_here - 1, 0)
    doc_here = lax.dynamic_slice_in_dim(group_document, group_here, 1, 1)[:, 0]
    doc_before = lax.dynamic_slice_in_dim(group_document, earlier, 1, 1)[:, 0]
    same_doc = (group_here >= 1) & (doc_here == doc_before)
    y_hi = lax.axis_index("mp") % 2
    scalars = jnp.concatenate([y_hi[None].astype(I32), same_doc.astype(I32)])
    whole = lambda *shape: pl.BlockSpec(shape, lambda i, s: (0,) * len(shape))
    query = pl.pallas_call(
        functools.partial(project_kernel, run),
        grid=(across_x // 2,),
        in_specs=[
            pl.BlockSpec((seqs, length, 4 * feats), lambda i: (0, 0, i)),
            pl.BlockSpec((seqs, 4 * feats), lambda i: (0, i)),
            pl.BlockSpec((4 * feats, cols), lambda i: (i, 2)),
        ],
        out_specs=pl.BlockSpec((seqs * length, cols), lambda i: (0, 0)),
        out_shape=jax.ShapeDtypeStruct((seqs * length, cols), BF),
        scratch_shapes=[pltpu.VMEM((seqs * length, cols), F32)],
        compiler_params=PARAMS,
    )(tokens, last_row, weights)

    def block(i, s):
        return 4 * (i % 2) + s[0] + (i // 2) * (1 - 2 * s[0])

    att, dquery = pl.pallas_call(
        functools.partial(attend_kernel, run),
        grid_spec=pltpu.PrefetchScalarGridSpec(
            num_scalar_prefetch=1,
            grid=(across_x,),
            in_specs=[
                whole(seqs * length, cols),
                pl.BlockSpec((2, id_count, feats), lambda i, s: (jnp.minimum(i, 1), 0, 0)),
                pl.BlockSpec((2, id_count, feats), lambda i, s: (jnp.maximum(i - 2, 0), 0, 0)),
                pl.BlockSpec((feats, 2 * cols), lambda i, s: (block(i, s), 0)),
                pl.BlockSpec((feats, 2 * cols), lambda i, s: (block(i, s) + 2, 0)),
                whole(seqs, length, cols),
                pl.BlockSpec((seqs, cols), lambda i, s: (0, width // cols)),
            ],
            out_specs=[whole(seqs, length, cols), whole(seqs, length, cols)],
            scratch_shapes=[pltpu.VMEM((id_count, 2 * cols), F32)],
        ),
        out_shape=[jax.ShapeDtypeStruct((seqs, length, cols), BF)] * 2,
        compiler_params=PARAMS,
    )(scalars, query, encoded, encoded_other, weights, weights, attended_grad, last_row)

    last = lax.ppermute(
        jnp.concatenate([att[:, -1], dquery[:, -1]], axis=-1), "group", backward
    )
    fixed = lambda *shape: pl.BlockSpec(shape, lambda i: (0,) * len(shape))
    attended, part = pl.pallas_call(
        functools.partial(token_kernel, run),
        grid=(1,),
        in_specs=[
            fixed(seqs, length, cols),
            fixed(seqs, length, cols),
            fixed(seqs, 2 * cols),
            pl.BlockSpec((width, cols), lambda i: (0, 2)),
        ],
        out_specs=[fixed(seqs, length, cols), fixed(mp_size, seqs * length, feats)],
        out_shape=[
            jax.ShapeDtypeStruct((seqs, length, cols), BF),
            jax.ShapeDtypeStruct((mp_size, seqs * length, feats), BF),
        ],
        compiler_params=PARAMS,
    )(att, dquery, last, weights)
    part = lax.all_to_all(part, "mp", split_axis=0, concat_axis=0, tiled=True)
    part = pl.pallas_call(
        sum_kernel,
        out_shape=jax.ShapeDtypeStruct((mp_size, seqs * length, feats), BF),
        compiler_params=PARAMS,
    )(part)
    part = lax.all_to_all(part, "mp", split_axis=0, concat_axis=0, tiled=True)
    token_grad = pl.pallas_call(
        join_kernel,
        grid=(mp_size // 2,),
        in_specs=[pl.BlockSpec((2, seqs * length, feats), lambda i: (i, 0, 0))],
        out_specs=pl.BlockSpec((seqs * length, 2 * feats), lambda i: (0, i)),
        out_shape=jax.ShapeDtypeStruct((seqs * length, width), BF),
        compiler_params=PARAMS,
    )(part)
    return (attended, token_grad.reshape(seqs, length, width))


def solution(mesh):
    in_specs = (
        P(None, "group", None),
        P("group", None, None),
        P(),
        P("group", "mp"),
        P("group", "mp"),
        P("group", "mp"),
        P("group", "mp"),
        P(None, "group", "mp"),
    )
    out_specs = (P(None, "group", "mp"), P(None, "group", None))
    return jax.shard_map(local, mesh=mesh, in_specs=in_specs, out_specs=out_specs, check_vma=False)
```

```python
import functools

import jax
import jax.numpy as jnp
from jax import lax
from jax.experimental import pallas as pl
from jax.experimental.pallas import tpu as pltpu
from jax.sharding import PartitionSpec as P

HEAD_DIM = 128
BF, F32, I32 = jnp.bfloat16, jnp.float32, jnp.int32
PARAMS = pltpu.CompilerParams(vmem_limit_bytes=48 * 1024 * 1024)
NT = (((1,), (1,)), ((), ()))


def iota(shape, dim):
    return lax.broadcasted_iota(I32, shape, dim)


def dot(a, b, dims=(((1,), (0,)), ((), ()))):
    return lax.dot_general(a, b, dims, preferred_element_type=F32)


def bucket_kernel(nchunk, rows_dev, ids_ref, requests_ref, slot_ref):
    seqs, keys = ids_ref.shape
    ids = jnp.concatenate([ids_ref[s : s + 1, :] for s in range(seqs)], axis=1)
    total = seqs * keys
    owner = ids // rows_dev
    lid = ids - owner * rows_dev
    owned = (iota((nchunk, total), 0) == owner).astype(F32)
    owned_bf = owned.astype(BF)
    earlier = (iota((total, total), 0) < iota((total, total), 1)).astype(F32).astype(BF)
    rank = jnp.sum(dot(owned_bf, earlier) * owned, axis=0, keepdims=True).astype(I32)
    placed = iota((128, total), 0) == rank
    high = jnp.where(placed, lid // 32, 0).astype(F32).astype(BF)
    low = jnp.where(placed, lid % 32, 0).astype(F32).astype(BF)
    requests_ref[...] = (dot(owned_bf, high, NT) * 32.0 + dot(owned_bf, low, NT)).astype(I32)
    slot = rank * nchunk + owner
    for s in range(seqs):
        slot_ref[s : s + 1, :] = slot[:, s * keys : (s + 1) * keys]


def fetch_kernel(capacity, asked_ref, table_ref, out_ref):
    nchunk = asked_ref.shape[0]
    rows_dev, feats = table_ref.shape
    asked = pltpu.roll(asked_ref[...], 1, 0)
    lanes = iota((nchunk, rows_dev), 1)
    chosen = jnp.concatenate(
        [(asked[:, s : s + 1] == lanes).astype(F32).astype(BF) for s in range(capacity)], axis=0
    )
    found = dot(chosen, table_ref[...]).astype(BF)
    for s in range(capacity):
        out_ref[:, s * feats : (s + 1) * feats] = found[s * nchunk : (s + 1) * nchunk]


def order_kernel(capacity, slot_ref, rows_ref, one_ref, out_ref):
    seqs, keys = slot_ref.shape
    nchunk = rows_ref.shape[0]
    copies, _, feats = out_ref.shape
    rows = jnp.concatenate(
        [rows_ref[:, s * feats : (s + 1) * feats] for s in range(capacity)], axis=0
    )
    slots = jnp.concatenate([slot_ref[...], jnp.zeros((8 - seqs, keys), I32)], axis=0)
    slots = slots.astype(F32).T.astype(I32)
    lanes = iota((keys, capacity * nchunk), 1)
    for s in range(seqs):
        chosen = (slots[:, s : s + 1] == lanes).astype(F32).astype(BF)
        found = dot(chosen, rows).astype(BF)
        if s < seqs - 1:
            one_ref[s * keys : (s + 1) * keys, :] = found
        for c in range(copies):
            out_ref[c, s * keys : (s + 1) * keys, :] = found


def in_order(weights, run):
    starts = [quad + turn * run for quad in range(0, weights.shape[0], 4 * run) for turn in (0, 2, 1, 3)]
    return jnp.concatenate([weights[start : start + run] for start in starts], axis=0)


def copies_kernel(in_ref, out_ref):
    for c in range(out_ref.shape[0]):
        out_ref[c] = in_ref[...]


def project_kernel(run, tok_ref, last_tok_ref, q_w_ref, q_ref, q_acc):
    step, steps = pl.program_id(0), pl.num_programs(0)
    seqs, length, deep = tok_ref.shape

    @pl.when(step == 0)
    def _():
        q_acc[...] = jnp.zeros_like(q_acc)

    is_last = iota((length, deep), 0) == length - 1
    tok = jnp.concatenate(
        [jnp.where(is_last, last_tok_ref[s : s + 1, :], tok_ref[s]) for s in range(seqs)], axis=0
    )
    q_acc[...] += dot(tok, in_order(q_w_ref[...], run))

    @pl.when(step == steps - 1)
    def _():
        q_ref[...] = q_acc[...].astype(BF)


def attend_kernel(
    run, scal_ref, q_ref, enc_ref, other_ref, other_last_ref, w_ref, next_w_ref, grad_ref, last_grad_ref,
    att_ref, dq_ref, kv_acc,
):
    step, steps = pl.program_id(0), pl.num_programs(0)
    seqs, length, cols = grad_ref.shape
    keys = kv_acc.shape[0] // seqs

    @pl.when(step == 0)
    def _():
        kv_acc[...] = jnp.zeros_like(kv_acc)

    def add(*refs):
        enc = [jnp.concatenate([ref[0], ref[1]], axis=1) for ref in refs]
        enc = jnp.concatenate(enc, axis=0)
        weights = jnp.concatenate([in_order(w_ref[...], run), in_order(next_w_ref[...], run)], axis=0)
        kv_acc[...] += dot(enc, weights)

    @pl.when(step < steps // 2)
    def _():
        add(enc_ref)

    @pl.when(step >= steps // 2)
    def _():
        add(other_ref, other_last_ref)

    @pl.when(step == steps - 1)
    def _():
        scale = HEAD_DIM ** (-0.5)
        kv, q = kv_acc[...].astype(BF), q_ref[...]
        last_row = iota((length, HEAD_DIM), 0) == length - 1
        units = [(s, h * HEAD_DIM) for s in range(seqs) for h in range(cols // HEAD_DIM)]
        valid = [last_row | (scal_ref[1 + s] != 0) for s in range(seqs)]
        query = [q[s * length : (s + 1) * length, h : h + HEAD_DIM] for s, h in units]
        key = [kv[s * keys : (s + 1) * keys, h : h + HEAD_DIM] for s, h in units]
        value = [kv[s * keys : (s + 1) * keys, cols + h : cols + h + HEAD_DIM] for s, h in units]
        grad = []
        for s, h in units:
            own = grad_ref[s, :, h : h + HEAD_DIM]
            own = jnp.where(last_row, last_grad_ref[s : s + 1, h : h + HEAD_DIM], own)
            grad.append(jnp.where(valid[s], own, jnp.zeros_like(own)))
        scores = jnp.concatenate([dot(a, b, NT) for a, b in zip(query, key)], axis=0) * scale
        prob_grad = jnp.concatenate([dot(a, b, NT) for a, b in zip(grad, value)], axis=0)
        exps = jnp.exp(scores - jnp.max(scores, axis=-1, keepdims=True))
        prob = exps / jnp.sum(exps, axis=-1, keepdims=True)
        prob_bf = prob.astype(BF)
        mean = jnp.sum(prob * prob_grad, axis=-1, keepdims=True)
        dscore = (prob * (prob_grad - mean) * scale).astype(BF)
        for i, (s, h) in enumerate(units):
            rows = slice(i * length, (i + 1) * length)
            mixed = dot(prob_bf[rows], value[i])
            att_ref[s, :, h : h + HEAD_DIM] = jnp.where(valid[s], mixed, 0.0).astype(BF)
            dq_ref[s, :, h : h + HEAD_DIM] = dot(dscore[rows], key[i]).astype(BF)


def token_kernel(run, att_ref, dq_ref, last_ref, w_ref, att_out, part_ref):
    seqs, length, cols = att_ref.shape
    blocks, _, feats = part_ref.shape
    is_last = iota((length, cols), 0) == length - 1
    rows = jnp.concatenate(
        [jnp.where(is_last, last_ref[s : s + 1, cols:], dq_ref[s]) for s in range(seqs)], axis=0
    )
    for c in range(blocks):
        weights = in_order(w_ref[c * feats : (c + 1) * feats], run)
        part_ref[c] = dot(rows, weights, NT).astype(BF)
    for s in range(seqs):
        att_out[s] = jnp.where(is_last, last_ref[s : s + 1, :cols], att_ref[s])


def sum_kernel(in_ref, out_ref):
    total = in_ref[0].astype(F32)
    for c in range(1, in_ref.shape[0]):
        total = total + in_ref[c].astype(F32)
    rounded = total.astype(BF)
    for c in range(out_ref.shape[0]):
        out_ref[c] = rounded


def join_kernel(in_ref, out_ref):
    feats = in_ref.shape[2]
    for c in range(in_ref.shape[0]):
        out_ref[:, c * feats : (c + 1) * feats] = in_ref[c]


def after(value, *earlier):
    return lax.optimization_barrier((value, earlier))[0]


def local(
    tokens, neighbour_ids, group_document, embed_table, w_query, w_key, w_value, attended_grad
):
    nchunk = lax.axis_size("group")
    mp_size = lax.axis_size("mp")
    group_here = lax.axis_index("group")
    seqs, length, width = tokens.shape
    run, cols = w_query.shape
    keys = neighbour_ids.shape[2]
    id_count = seqs * keys
    rows_dev, feats = embed_table.shape
    capacity = max(2, 3 * id_count // (2 * nchunk))
    onward = [(g, (g + 1) % nchunk) for g in range(nchunk)]
    backward = [(g, (g - 1) % nchunk) for g in range(nchunk)]

    def paired(own, near):
        lower = (group_here // 2) % 2 == 0
        return jnp.concatenate([jnp.where(lower, own, near), jnp.where(lower, near, own)], axis=0)

    def round_z(value):
        groups = [
            [z * 4 + y * 2 + c for z in range(nchunk // 4) for c in range(2)] for y in range(2)
        ]
        return lax.all_gather(value, "group", axis=0, tiled=True, axis_index_groups=groups)

    zero = jnp.zeros((), BF)
    own = sum(
        lax.pad(block, zero, ((0, 0, 0), (i * cols, (2 - i) * cols, 0)))
        for i, block in enumerate((w_key, w_value, w_query))
    )
    pair = paired(own, lax.ppermute(own, "group", [(g, g ^ 2) for g in range(nchunk)]))

    last_row = lax.ppermute(
        jnp.concatenate([tokens[:, -1], attended_grad[:, -1]], axis=1), "group", onward
    )

    requests, slot = pl.pallas_call(
        functools.partial(bucket_kernel, nchunk, rows_dev),
        out_shape=[
            jax.ShapeDtypeStruct((nchunk, 128), I32),
            jax.ShapeDtypeStruct((seqs, keys), I32),
        ],
        compiler_params=PARAMS,
    )(neighbour_ids.reshape(seqs, keys))
    slot = lax.ppermute(slot, "group", onward)
    asked = lax.all_to_all(requests, "group", split_axis=0, concat_axis=0, tiled=True)
    weights = round_z(after(pair, asked))
    found = pl.pallas_call(
        functools.partial(fetch_kernel, capacity),
        out_shape=jax.ShapeDtypeStruct((nchunk, capacity * feats), BF),
        compiler_params=PARAMS,
    )(asked, embed_table)
    found = found.reshape(nchunk, 2, -1)
    returned = lax.all_to_all(found, "group", split_axis=0, concat_axis=0, tiled=True)
    returned = after(returned.reshape(nchunk, -1), last_row)
    across_x = mp_size // 2
    along_x = [[2 * x + y for x in range(across_x)] for y in range(2)]
    copies = jax.ShapeDtypeStruct((across_x, id_count, feats), BF)

    def round_x(value):
        return lax.all_to_all(
            value, "mp", split_axis=0, concat_axis=0, tiled=True, axis_index_groups=along_x
        )

    single, encoded = pl.pallas_call(
        functools.partial(order_kernel, capacity),
        out_shape=[jax.ShapeDtypeStruct((id_count - keys, feats), BF), copies],
        compiler_params=PARAMS,
    )(slot, returned)
    single = lax.ppermute(single, "mp", [(m, m ^ 1) for m in range(mp_size)])
    encoded = round_x(encoded)
    encoded_last = lax.ppermute(
        encoded[:, id_count - keys :], "mp", [(m, m ^ 1) for m in range(mp_size)]
    )
    encoded_other = round_x(
        pl.pallas_call(
            copies_kernel,
            out_shape=jax.ShapeDtypeStruct((across_x, id_count - keys, feats), BF),
            compiler_params=PARAMS,
        )(single)
    )

    earlier = jnp.maximum(group_here - 1, 0)
    doc_here = lax.dynamic_slice_in_dim(group_document, group_here, 1, 1)[:, 0]
    doc_before = lax.dynamic_slice_in_dim(group_document, earlier, 1, 1)[:, 0]
    same_doc = (group_here >= 1) & (doc_here == doc_before)
    y_hi = lax.axis_index("mp") % 2
    scalars = jnp.concatenate([y_hi[None].astype(I32), same_doc.astype(I32)])
    whole = lambda *shape: pl.BlockSpec(shape, lambda i, s: (0,) * len(shape))
    query = pl.pallas_call(
        functools.partial(project_kernel, run),
        grid=(across_x // 2,),
        in_specs=[
            pl.BlockSpec((seqs, length, 4 * feats), lambda i: (0, 0, i)),
            pl.BlockSpec((seqs, 4 * feats), lambda i: (0, i)),
            pl.BlockSpec((4 * feats, cols), lambda i: (i, 2)),
        ],
        out_specs=pl.BlockSpec((seqs * length, cols), lambda i: (0, 0)),
        out_shape=jax.ShapeDtypeStruct((seqs * length, cols), BF),
        scratch_shapes=[pltpu.VMEM((seqs * length, cols), F32)],
        compiler_params=PARAMS,
    )(tokens, last_row, weights)

    def block(i, s):
        return 4 * (i % 2) + s[0] + (i // 2) * (1 - 2 * s[0])

    att, dquery = pl.pallas_call(
        functools.partial(attend_kernel, run),
        grid_spec=pltpu.PrefetchScalarGridSpec(
            num_scalar_prefetch=1,
            grid=(across_x,),
            in_specs=[
                whole(seqs * length, cols),
                pl.BlockSpec((2, id_count, feats), lambda i, s: (jnp.minimum(i, 1), 0, 0)),
                pl.BlockSpec((2, id_count - keys, feats), lambda i, s: (jnp.maximum(i - 2, 0), 0, 0)),
                pl.BlockSpec((2, keys, feats), lambda i, s: (jnp.maximum(i - 2, 0), 0, 0)),
                pl.BlockSpec((feats, 2 * cols), lambda i, s: (block(i, s), 0)),
                pl.BlockSpec((feats, 2 * cols), lambda i, s: (block(i, s) + 2, 0)),
                whole(seqs, length, cols),
                pl.BlockSpec((seqs, cols), lambda i, s: (0, width // cols)),
            ],
            out_specs=[whole(seqs, length, cols), whole(seqs, length, cols)],
            scratch_shapes=[pltpu.VMEM((id_count, 2 * cols), F32)],
        ),
        out_shape=[jax.ShapeDtypeStruct((seqs, length, cols), BF)] * 2,
        compiler_params=PARAMS,
    )(scalars, query, encoded, encoded_other, encoded_last, weights, weights, attended_grad, last_row)

    last = lax.ppermute(
        jnp.concatenate([att[:, -1], dquery[:, -1]], axis=-1), "group", backward
    )
    fixed = lambda *shape: pl.BlockSpec(shape, lambda i: (0,) * len(shape))
    attended, part = pl.pallas_call(
        functools.partial(token_kernel, run),
        grid=(1,),
        in_specs=[
            fixed(seqs, length, cols),
            fixed(seqs, length, cols),
            fixed(seqs, 2 * cols),
            pl.BlockSpec((width, cols), lambda i: (0, 2)),
        ],
        out_specs=[fixed(seqs, length, cols), fixed(mp_size, seqs * length, feats)],
        out_shape=[
            jax.ShapeDtypeStruct((seqs, length, cols), BF),
            jax.ShapeDtypeStruct((mp_size, seqs * length, feats), BF),
        ],
        compiler_params=PARAMS,
    )(att, dquery, last, weights)
    part = lax.all_to_all(part, "mp", split_axis=0, concat_axis=0, tiled=True)
    part = pl.pallas_call(
        sum_kernel,
        out_shape=jax.ShapeDtypeStruct((mp_size, seqs * length, feats), BF),
        compiler_params=PARAMS,
    )(part)
    part = lax.all_to_all(part, "mp", split_axis=0, concat_axis=0, tiled=True)
    token_grad = pl.pallas_call(
        join_kernel,
        grid=(mp_size // 2,),
        in_specs=[pl.BlockSpec((2, seqs * length, feats), lambda i: (i, 0, 0))],
        out_specs=pl.BlockSpec((seqs * length, 2 * feats), lambda i: (0, i)),
        out_shape=jax.ShapeDtypeStruct((seqs * length, width), BF),
        compiler_params=PARAMS,
    )(part)
    return (attended, token_grad.reshape(seqs, length, width))


def solution(mesh):
    in_specs = (
        P(None, "group", None),
        P("group", None, None),
        P(),
        P("group", "mp"),
        P("group", "mp"),
        P("group", "mp"),
        P("group", "mp"),
        P(None, "group", "mp"),
    )
    out_specs = (P(None, "group", "mp"), P(None, "group", None))
    return jax.shard_map(local, mesh=mesh, in_specs=in_specs, out_specs=out_specs, check_vma=False)
```

```python
import functools

import jax
import jax.numpy as jnp
from jax import lax
from jax.experimental import pallas as pl
from jax.experimental.pallas import tpu as pltpu
from jax.sharding import PartitionSpec as P

HEAD_DIM = 128
BF, F32, I32 = jnp.bfloat16, jnp.float32, jnp.int32
PARAMS = pltpu.CompilerParams(vmem_limit_bytes=48 * 1024 * 1024)
ROOMY = pltpu.CompilerParams(vmem_limit_bytes=60 * 1024 * 1024)
NT = (((1,), (1,)), ((), ()))


def iota(shape, dim):
    return lax.broadcasted_iota(I32, shape, dim)


def dot(a, b, dims=(((1,), (0,)), ((), ()))):
    return lax.dot_general(a, b, dims, preferred_element_type=F32)


def bucket_kernel(nchunk, rows_dev, ids_ref, requests_ref, slot_ref):
    seqs, keys = ids_ref.shape
    ids = jnp.concatenate([ids_ref[s : s + 1, :] for s in range(seqs)], axis=1)
    total = seqs * keys
    owner = ids // rows_dev
    lid = ids - owner * rows_dev
    owned = (iota((nchunk, total), 0) == owner).astype(F32)
    owned_bf = owned.astype(BF)
    earlier = (iota((total, total), 0) < iota((total, total), 1)).astype(F32).astype(BF)
    rank = jnp.sum(dot(owned_bf, earlier) * owned, axis=0, keepdims=True).astype(I32)
    placed = iota((128, total), 0) == rank
    high = jnp.where(placed, lid // 32, 0).astype(F32).astype(BF)
    low = jnp.where(placed, lid % 32, 0).astype(F32).astype(BF)
    requests_ref[...] = (dot(owned_bf, high, NT) * 32.0 + dot(owned_bf, low, NT)).astype(I32)
    slot = rank * nchunk + owner
    for s in range(seqs):
        slot_ref[s : s + 1, :] = slot[:, s * keys : (s + 1) * keys]


def fetch_kernel(capacity, asked_ref, table_ref, out_ref):
    nchunk = asked_ref.shape[0]
    rows_dev, feats = table_ref.shape
    asked = pltpu.roll(asked_ref[...], 1, 0)
    lanes = iota((nchunk, rows_dev), 1)
    chosen = jnp.concatenate(
        [(asked[:, s : s + 1] == lanes).astype(F32).astype(BF) for s in range(capacity)], axis=0
    )
    found = dot(chosen, table_ref[...]).astype(BF)
    for s in range(capacity):
        out_ref[:, s * feats : (s + 1) * feats] = found[s * nchunk : (s + 1) * nchunk]


def order_kernel(capacity, slot_ref, rows_ref, one_ref, out_ref):
    seqs, keys = slot_ref.shape
    nchunk = rows_ref.shape[0]
    copies, _, feats = out_ref.shape
    rows = jnp.concatenate(
        [rows_ref[:, s * feats : (s + 1) * feats] for s in range(capacity)], axis=0
    )
    slots = jnp.concatenate([slot_ref[...], jnp.zeros((8 - seqs, keys), I32)], axis=0)
    slots = slots.astype(F32).T.astype(I32)
    lanes = iota((keys, capacity * nchunk), 1)
    for s in range(seqs):
        chosen = (slots[:, s : s + 1] == lanes).astype(F32).astype(BF)
        found = dot(chosen, rows).astype(BF)
        if s < seqs - 1:
            one_ref[s * keys : (s + 1) * keys, :] = found
        for c in range(copies):
            out_ref[c, s * keys : (s + 1) * keys, :] = found


def in_order(weights, run):
    starts = [quad + turn * run for quad in range(0, weights.shape[0], 4 * run) for turn in (0, 2, 1, 3)]
    return jnp.concatenate([weights[start : start + run] for start in starts], axis=0)


def copies_kernel(in_ref, out_ref):
    for c in range(out_ref.shape[0]):
        out_ref[c] = in_ref[...]


def project_kernel(run, tok_ref, last_tok_ref, q_w_ref, q_ref, q_acc):
    step, steps = pl.program_id(0), pl.num_programs(0)
    seqs, length, deep = tok_ref.shape

    @pl.when(step == 0)
    def _():
        q_acc[...] = jnp.zeros_like(q_acc)

    is_last = iota((length, deep), 0) == length - 1
    tok = jnp.concatenate(
        [jnp.where(is_last, last_tok_ref[s : s + 1, :], tok_ref[s]) for s in range(seqs)], axis=0
    )
    q_acc[...] += dot(tok, in_order(q_w_ref[...], run))

    @pl.when(step == steps - 1)
    def _():
        q_ref[...] = q_acc[...].astype(BF)


def attend_kernel(
    run, scal_ref, q_ref, enc_ref, other_ref, other_last_ref, w_ref, next_w_ref, grad_ref, last_grad_ref,
    att_ref, dq_ref, kv_acc,
):
    step, steps = pl.program_id(0), pl.num_programs(0)
    seqs, length, cols = grad_ref.shape
    keys = kv_acc.shape[0] // seqs

    @pl.when(step == 0)
    def _():
        kv_acc[...] = jnp.zeros_like(kv_acc)

    def add(*refs):
        enc = [jnp.concatenate([ref[0], ref[1]], axis=1) for ref in refs]
        enc = jnp.concatenate(enc, axis=0)
        weights = jnp.concatenate([in_order(w_ref[...], run), in_order(next_w_ref[...], run)], axis=0)
        kv_acc[...] += dot(enc, weights)

    @pl.when(step < steps // 2)
    def _():
        add(enc_ref)

    @pl.when(step >= steps // 2)
    def _():
        add(other_ref, other_last_ref)

    @pl.when(step == steps - 1)
    def _():
        scale = HEAD_DIM ** (-0.5)
        kv, q = kv_acc[...].astype(BF), q_ref[...]
        last_row = iota((length, HEAD_DIM), 0) == length - 1
        units = [(s, h * HEAD_DIM) for s in range(seqs) for h in range(cols // HEAD_DIM)]
        valid = [last_row | (scal_ref[1 + s] != 0) for s in range(seqs)]
        query = [q[s * length : (s + 1) * length, h : h + HEAD_DIM] for s, h in units]
        key = [kv[s * keys : (s + 1) * keys, h : h + HEAD_DIM] for s, h in units]
        value = [kv[s * keys : (s + 1) * keys, cols + h : cols + h + HEAD_DIM] for s, h in units]
        grad = []
        for s, h in units:
            own = grad_ref[s, :, h : h + HEAD_DIM]
            own = jnp.where(last_row, last_grad_ref[s : s + 1, h : h + HEAD_DIM], own)
            grad.append(jnp.where(valid[s], own, jnp.zeros_like(own)))
        scores = jnp.concatenate([dot(a, b, NT) for a, b in zip(query, key)], axis=0) * scale
        prob_grad = jnp.concatenate([dot(a, b, NT) for a, b in zip(grad, value)], axis=0)
        exps = jnp.exp(scores - jnp.max(scores, axis=-1, keepdims=True))
        prob = exps / jnp.sum(exps, axis=-1, keepdims=True)
        prob_bf = prob.astype(BF)
        mean = jnp.sum(prob * prob_grad, axis=-1, keepdims=True)
        dscore = (prob * (prob_grad - mean) * scale).astype(BF)
        for i, (s, h) in enumerate(units):
            rows = slice(i * length, (i + 1) * length)
            mixed = dot(prob_bf[rows], value[i])
            att_ref[s, :, h : h + HEAD_DIM] = jnp.where(valid[s], mixed, 0.0).astype(BF)
            dq_ref[s, :, h : h + HEAD_DIM] = dot(dscore[rows], key[i]).astype(BF)


def token_kernel(run, att_ref, dq_ref, last_ref, w_ref, att_out, part_ref):
    seqs, length, cols = att_ref.shape
    blocks, _, feats = part_ref.shape
    is_last = iota((length, cols), 0) == length - 1
    rows = jnp.concatenate(
        [jnp.where(is_last, last_ref[s : s + 1, cols:], dq_ref[s]) for s in range(seqs)], axis=0
    )
    for c in range(blocks):
        weights = in_order(w_ref[c * feats : (c + 1) * feats], run)
        part_ref[c] = dot(rows, weights, NT).astype(BF)
    for s in range(seqs):
        att_out[s] = jnp.where(is_last, last_ref[s : s + 1, :cols], att_ref[s])


def sum_kernel(in_ref, out_ref):
    total = in_ref[0].astype(F32)
    for c in range(1, in_ref.shape[0]):
        total = total + in_ref[c].astype(F32)
    rounded = total.astype(BF)
    for c in range(out_ref.shape[0]):
        out_ref[c] = rounded


def join_kernel(in_ref, out_ref):
    feats = in_ref.shape[2]
    for c in range(in_ref.shape[0]):
        out_ref[:, c * feats : (c + 1) * feats] = in_ref[c]


def after(value, *earlier):
    return lax.optimization_barrier((value, earlier))[0]


def local(
    tokens, neighbour_ids, group_document, embed_table, w_query, w_key, w_value, attended_grad
):
    nchunk = lax.axis_size("group")
    mp_size = lax.axis_size("mp")
    group_here = lax.axis_index("group")
    seqs, length, width = tokens.shape
    run, cols = w_query.shape
    keys = neighbour_ids.shape[2]
    id_count = seqs * keys
    rows_dev, feats = embed_table.shape
    capacity = max(2, 3 * id_count // (2 * nchunk))
    onward = [(g, (g + 1) % nchunk) for g in range(nchunk)]
    backward = [(g, (g - 1) % nchunk) for g in range(nchunk)]

    def paired(own, near):
        lower = (group_here // 2) % 2 == 0
        return jnp.concatenate([jnp.where(lower, own, near), jnp.where(lower, near, own)], axis=0)

    def round_z(value):
        groups = [
            [z * 4 + y * 2 + c for z in range(nchunk // 4) for c in range(2)] for y in range(2)
        ]
        return lax.all_gather(value, "group", axis=0, tiled=True, axis_index_groups=groups)

    zero = jnp.zeros((), BF)
    own = sum(
        lax.pad(block, zero, ((0, 0, 0), (i * cols, (2 - i) * cols, 0)))
        for i, block in enumerate((w_key, w_value, w_query))
    )
    pair = paired(own, lax.ppermute(own, "group", [(g, g ^ 2) for g in range(nchunk)]))

    last_row = lax.ppermute(
        jnp.concatenate([tokens[:, -1], attended_grad[:, -1]], axis=1), "group", onward
    )

    requests, slot = pl.pallas_call(
        functools.partial(bucket_kernel, nchunk, rows_dev),
        out_shape=[
            jax.ShapeDtypeStruct((nchunk, 128), I32),
            jax.ShapeDtypeStruct((seqs, keys), I32),
        ],
        compiler_params=PARAMS,
    )(neighbour_ids.reshape(seqs, keys))
    slot = lax.ppermute(slot, "group", onward)
    asked = lax.all_to_all(requests, "group", split_axis=0, concat_axis=0, tiled=True)
    weights = round_z(after(pair, asked))
    found = pl.pallas_call(
        functools.partial(fetch_kernel, capacity),
        out_shape=jax.ShapeDtypeStruct((nchunk, capacity * feats), BF),
        compiler_params=PARAMS,
    )(asked, embed_table)
    found = found.reshape(nchunk, 2, -1)
    returned = lax.all_to_all(found, "group", split_axis=0, concat_axis=0, tiled=True)
    returned = after(returned.reshape(nchunk, -1), last_row)
    across_x = mp_size // 2
    along_x = [[2 * x + y for x in range(across_x)] for y in range(2)]
    copies = jax.ShapeDtypeStruct((across_x, id_count, feats), BF)

    def round_x(value):
        return lax.all_to_all(
            value, "mp", split_axis=0, concat_axis=0, tiled=True, axis_index_groups=along_x
        )

    single, encoded = pl.pallas_call(
        functools.partial(order_kernel, capacity),
        out_shape=[jax.ShapeDtypeStruct((id_count - keys, feats), BF), copies],
        compiler_params=PARAMS,
    )(slot, returned)
    single = lax.ppermute(single, "mp", [(m, m ^ 1) for m in range(mp_size)])
    encoded = round_x(encoded)
    encoded_last = lax.ppermute(
        encoded[:, id_count - keys :], "mp", [(m, m ^ 1) for m in range(mp_size)]
    )
    encoded_other = round_x(
        pl.pallas_call(
            copies_kernel,
            out_shape=jax.ShapeDtypeStruct((across_x, id_count - keys, feats), BF),
            compiler_params=PARAMS,
        )(single)
    )

    earlier = jnp.maximum(group_here - 1, 0)
    doc_here = lax.dynamic_slice_in_dim(group_document, group_here, 1, 1)[:, 0]
    doc_before = lax.dynamic_slice_in_dim(group_document, earlier, 1, 1)[:, 0]
    same_doc = (group_here >= 1) & (doc_here == doc_before)
    y_hi = lax.axis_index("mp") % 2
    scalars = jnp.concatenate([y_hi[None].astype(I32), same_doc.astype(I32)])
    whole = lambda *shape: pl.BlockSpec(shape, lambda i, s: (0,) * len(shape))
    query = pl.pallas_call(
        functools.partial(project_kernel, run),
        grid=(across_x,),
        in_specs=[
            pl.BlockSpec((seqs, length, 2 * feats), lambda i: (0, 0, i)),
            pl.BlockSpec((seqs, 2 * feats), lambda i: (0, i)),
            pl.BlockSpec((2 * feats, cols), lambda i: (i, 2)),
        ],
        out_specs=pl.BlockSpec((seqs * length, cols), lambda i: (0, 0)),
        out_shape=jax.ShapeDtypeStruct((seqs * length, cols), BF),
        scratch_shapes=[pltpu.VMEM((seqs * length, cols), F32)],
        compiler_params=ROOMY,
    )(tokens, last_row, weights)

    def block(i, s):
        return 4 * (i % 2) + s[0] + (i // 2) * (1 - 2 * s[0])

    att, dquery = pl.pallas_call(
        functools.partial(attend_kernel, run),
        grid_spec=pltpu.PrefetchScalarGridSpec(
            num_scalar_prefetch=1,
            grid=(across_x,),
            in_specs=[
                whole(seqs * length, cols),
                pl.BlockSpec((2, id_count, feats), lambda i, s: (jnp.minimum(i, 1), 0, 0)),
                pl.BlockSpec((2, id_count - keys, feats), lambda i, s: (jnp.maximum(i - 2, 0), 0, 0)),
                pl.BlockSpec((2, keys, feats), lambda i, s: (jnp.maximum(i - 2, 0), 0, 0)),
                pl.BlockSpec((feats, 2 * cols), lambda i, s: (block(i, s), 0)),
                pl.BlockSpec((feats, 2 * cols), lambda i, s: (block(i, s) + 2, 0)),
                whole(seqs, length, cols),
                pl.BlockSpec((seqs, cols), lambda i, s: (0, width // cols)),
            ],
            out_specs=[whole(seqs, length, cols), whole(seqs, length, cols)],
            scratch_shapes=[pltpu.VMEM((id_count, 2 * cols), F32)],
        ),
        out_shape=[jax.ShapeDtypeStruct((seqs, length, cols), BF)] * 2,
        compiler_params=PARAMS,
    )(scalars, query, encoded, encoded_other, encoded_last, weights, weights, attended_grad, last_row)

    last = lax.ppermute(
        jnp.concatenate([att[:, -1], dquery[:, -1]], axis=-1), "group", backward
    )
    fixed = lambda *shape: pl.BlockSpec(shape, lambda i: (0,) * len(shape))
    attended, part = pl.pallas_call(
        functools.partial(token_kernel, run),
        grid=(1,),
        in_specs=[
            fixed(seqs, length, cols),
            fixed(seqs, length, cols),
            fixed(seqs, 2 * cols),
            pl.BlockSpec((width, cols), lambda i: (0, 2)),
        ],
        out_specs=[fixed(seqs, length, cols), fixed(mp_size, seqs * length, feats)],
        out_shape=[
            jax.ShapeDtypeStruct((seqs, length, cols), BF),
            jax.ShapeDtypeStruct((mp_size, seqs * length, feats), BF),
        ],
        compiler_params=PARAMS,
    )(att, dquery, last, weights)
    part = lax.all_to_all(part, "mp", split_axis=0, concat_axis=0, tiled=True)
    part = pl.pallas_call(
        sum_kernel,
        out_shape=jax.ShapeDtypeStruct((mp_size, seqs * length, feats), BF),
        compiler_params=PARAMS,
    )(part)
    part = lax.all_to_all(part, "mp", split_axis=0, concat_axis=0, tiled=True)
    token_grad = pl.pallas_call(
        join_kernel,
        grid=(mp_size // 2,),
        in_specs=[pl.BlockSpec((2, seqs * length, feats), lambda i: (i, 0, 0))],
        out_specs=pl.BlockSpec((seqs * length, 2 * feats), lambda i: (0, i)),
        out_shape=jax.ShapeDtypeStruct((seqs * length, width), BF),
        compiler_params=PARAMS,
    )(part)
    return (attended, token_grad.reshape(seqs, length, width))


def solution(mesh):
    in_specs = (
        P(None, "group", None),
        P("group", None, None),
        P(),
        P("group", "mp"),
        P("group", "mp"),
        P("group", "mp"),
        P("group", "mp"),
        P(None, "group", "mp"),
    )
    out_specs = (P(None, "group", "mp"), P(None, "group", None))
    return jax.shard_map(local, mesh=mesh, in_specs=in_specs, out_specs=out_specs, check_vma=False)
```

```python
import functools

import jax
import jax.numpy as jnp
from jax import lax
from jax.experimental import pallas as pl
from jax.experimental.pallas import tpu as pltpu
from jax.sharding import PartitionSpec as P

HEAD_DIM = 128
BF, F32, I32 = jnp.bfloat16, jnp.float32, jnp.int32
PARAMS = pltpu.CompilerParams(vmem_limit_bytes=48 * 1024 * 1024)
NT = (((1,), (1,)), ((), ()))


def iota(shape, dim):
    return lax.broadcasted_iota(I32, shape, dim)


def dot(a, b, dims=(((1,), (0,)), ((), ()))):
    return lax.dot_general(a, b, dims, preferred_element_type=F32)


def bucket_kernel(nchunk, rows_dev, ids_ref, requests_ref, slot_ref):
    seqs, keys = ids_ref.shape
    ids = jnp.concatenate([ids_ref[s : s + 1, :] for s in range(seqs)], axis=1)
    total = seqs * keys
    owner = ids // rows_dev
    lid = ids - owner * rows_dev
    owned = (iota((nchunk, total), 0) == owner).astype(F32)
    owned_bf = owned.astype(BF)
    earlier = (iota((total, total), 0) < iota((total, total), 1)).astype(F32).astype(BF)
    rank = jnp.sum(dot(owned_bf, earlier) * owned, axis=0, keepdims=True).astype(I32)
    placed = iota((128, total), 0) == rank
    high = jnp.where(placed, lid // 32, 0).astype(F32).astype(BF)
    low = jnp.where(placed, lid % 32, 0).astype(F32).astype(BF)
    requests_ref[...] = (dot(owned_bf, high, NT) * 32.0 + dot(owned_bf, low, NT)).astype(I32)
    slot = rank * nchunk + owner
    for s in range(seqs):
        slot_ref[s : s + 1, :] = slot[:, s * keys : (s + 1) * keys]


def fetch_kernel(capacity, asked_ref, table_ref, out_ref):
    nchunk = asked_ref.shape[0]
    rows_dev, feats = table_ref.shape
    asked = pltpu.roll(asked_ref[...], 1, 0)
    lanes = iota((nchunk, rows_dev), 1)
    chosen = jnp.concatenate(
        [(asked[:, s : s + 1] == lanes).astype(F32).astype(BF) for s in range(capacity)], axis=0
    )
    found = dot(chosen, table_ref[...]).astype(BF)
    for s in range(capacity):
        out_ref[:, s * feats : (s + 1) * feats] = found[s * nchunk : (s + 1) * nchunk]


def order_kernel(capacity, slot_ref, rows_ref, one_ref, out_ref):
    seqs, keys = slot_ref.shape
    nchunk = rows_ref.shape[0]
    copies, _, feats = out_ref.shape
    rows = jnp.concatenate(
        [rows_ref[:, s * feats : (s + 1) * feats] for s in range(capacity)], axis=0
    )
    slots = jnp.concatenate([slot_ref[...], jnp.zeros((8 - seqs, keys), I32)], axis=0)
    slots = slots.astype(F32).T.astype(I32)
    lanes = iota((keys, capacity * nchunk), 1)
    for s in range(seqs):
        chosen = (slots[:, s : s + 1] == lanes).astype(F32).astype(BF)
        found = dot(chosen, rows).astype(BF)
        one_ref[s * keys : (s + 1) * keys, :] = found
        for c in range(copies):
            out_ref[c, s * keys : (s + 1) * keys, :] = found


def in_order(weights, run):
    starts = [quad + turn * run for quad in range(0, weights.shape[0], 4 * run) for turn in (0, 2, 1, 3)]
    return jnp.concatenate([weights[start : start + run] for start in starts], axis=0)


def copies_kernel(in_ref, out_ref):
    for c in range(out_ref.shape[0]):
        out_ref[c] = in_ref[...]


def project_kernel(
    run, scal_ref, enc_ref, w_ref, next_w_ref, tok_ref, last_tok_ref, q_w_ref, kv_ref, q_ref, kv_acc,
    q_acc,
):
    step, steps = pl.program_id(0), pl.num_programs(0)
    seqs, length, deep = tok_ref.shape

    @pl.when(step == 0)
    def _():
        kv_acc[...] = jnp.zeros_like(kv_acc)
        q_acc[...] = jnp.zeros_like(q_acc)

    is_last = iota((length, deep), 0) == length - 1
    tok = jnp.concatenate(
        [jnp.where(is_last, last_tok_ref[s : s + 1, :], tok_ref[s]) for s in range(seqs)], axis=0
    )
    enc = jnp.concatenate([enc_ref[0], enc_ref[1]], axis=1)
    weights = jnp.concatenate([in_order(w_ref[...], run), in_order(next_w_ref[...], run)], axis=0)
    kv_acc[...] += dot(enc, weights)
    q_acc[...] += dot(tok, in_order(q_w_ref[...], run))

    @pl.when(step == steps - 1)
    def _():
        kv_ref[...] = kv_acc[...]
        q_ref[...] = q_acc[...].astype(BF)


def attend_kernel(
    run, scal_ref, kv_ref, q_ref, enc_ref, w_ref, next_w_ref, grad_ref, last_grad_ref, att_ref, dq_ref,
    kv_acc,
):
    step, steps = pl.program_id(0), pl.num_programs(0)
    seqs, length, cols = grad_ref.shape
    keys = kv_acc.shape[0] // seqs

    @pl.when(step == 0)
    def _():
        kv_acc[...] = kv_ref[...]

    enc = jnp.concatenate([enc_ref[0], enc_ref[1]], axis=1)
    weights = jnp.concatenate([in_order(w_ref[...], run), in_order(next_w_ref[...], run)], axis=0)
    kv_acc[...] += dot(enc, weights)

    @pl.when(step == steps - 1)
    def _():
        scale = HEAD_DIM ** (-0.5)
        kv, q = kv_acc[...].astype(BF), q_ref[...]
        last_row = iota((length, HEAD_DIM), 0) == length - 1
        units = [(s, h * HEAD_DIM) for s in range(seqs) for h in range(cols // HEAD_DIM)]
        valid = [last_row | (scal_ref[1 + s] != 0) for s in range(seqs)]
        query = [q[s * length : (s + 1) * length, h : h + HEAD_DIM] for s, h in units]
        key = [kv[s * keys : (s + 1) * keys, h : h + HEAD_DIM] for s, h in units]
        value = [kv[s * keys : (s + 1) * keys, cols + h : cols + h + HEAD_DIM] for s, h in units]
        grad = []
        for s, h in units:
            own = grad_ref[s, :, h : h + HEAD_DIM]
            own = jnp.where(last_row, last_grad_ref[s : s + 1, h : h + HEAD_DIM], own)
            grad.append(jnp.where(valid[s], own, jnp.zeros_like(own)))
        scores = jnp.concatenate([dot(a, b, NT) for a, b in zip(query, key)], axis=0) * scale
        prob_grad = jnp.concatenate([dot(a, b, NT) for a, b in zip(grad, value)], axis=0)
        exps = jnp.exp(scores - jnp.max(scores, axis=-1, keepdims=True))
        prob = exps / jnp.sum(exps, axis=-1, keepdims=True)
        prob_bf = prob.astype(BF)
        mean = jnp.sum(prob * prob_grad, axis=-1, keepdims=True)
        dscore = (prob * (prob_grad - mean) * scale).astype(BF)
        for i, (s, h) in enumerate(units):
            rows = slice(i * length, (i + 1) * length)
            mixed = dot(prob_bf[rows], value[i])
            att_ref[s, :, h : h + HEAD_DIM] = jnp.where(valid[s], mixed, 0.0).astype(BF)
            dq_ref[s, :, h : h + HEAD_DIM] = dot(dscore[rows], key[i]).astype(BF)


def token_kernel(run, att_ref, dq_ref, last_ref, w_ref, att_out, part_ref):
    seqs, length, cols = att_ref.shape
    blocks, _, feats = part_ref.shape
    is_last = iota((length, cols), 0) == length - 1
    rows = jnp.concatenate(
        [jnp.where(is_last, last_ref[s : s + 1, cols:], dq_ref[s]) for s in range(seqs)], axis=0
    )
    for c in range(blocks):
        weights = in_order(w_ref[c * feats : (c + 1) * feats], run)
        part_ref[c] = dot(rows, weights, NT).astype(BF)
    for s in range(seqs):
        att_out[s] = jnp.where(is_last, last_ref[s : s + 1, :cols], att_ref[s])


def sum_kernel(in_ref, out_ref):
    total = in_ref[0].astype(F32)
    for c in range(1, in_ref.shape[0]):
        total = total + in_ref[c].astype(F32)
    rounded = total.astype(BF)
    for c in range(out_ref.shape[0]):
        out_ref[c] = rounded


def join_kernel(in_ref, out_ref):
    feats = in_ref.shape[2]
    for c in range(in_ref.shape[0]):
        out_ref[:, c * feats : (c + 1) * feats] = in_ref[c]


def after(value, *earlier):
    return lax.optimization_barrier((value, earlier))[0]


def local(
    tokens, neighbour_ids, group_document, embed_table, w_query, w_key, w_value, attended_grad
):
    nchunk = lax.axis_size("group")
    mp_size = lax.axis_size("mp")
    group_here = lax.axis_index("group")
    seqs, length, width = tokens.shape
    run, cols = w_query.shape
    keys = neighbour_ids.shape[2]
    id_count = seqs * keys
    rows_dev, feats = embed_table.shape
    capacity = max(2, 3 * id_count // (2 * nchunk))
    onward = [(g, (g + 1) % nchunk) for g in range(nchunk)]
    backward = [(g, (g - 1) % nchunk) for g in range(nchunk)]

    def paired(own, near):
        lower = (group_here // 2) % 2 == 0
        return jnp.concatenate([jnp.where(lower, own, near), jnp.where(lower, near, own)], axis=0)

    def round_z(value):
        groups = [
            [z * 4 + y * 2 + c for z in range(nchunk // 4) for c in range(2)] for y in range(2)
        ]
        return lax.all_gather(value, "group", axis=0, tiled=True, axis_index_groups=groups)

    zero = jnp.zeros((), BF)
    own = sum(
        lax.pad(block, zero, ((0, 0, 0), (i * cols, (2 - i) * cols, 0)))
        for i, block in enumerate((w_key, w_value, w_query))
    )
    pair = paired(own, lax.ppermute(own, "group", [(g, g ^ 2) for g in range(nchunk)]))

    last_row = lax.ppermute(
        jnp.concatenate([tokens[:, -1], attended_grad[:, -1]], axis=1), "group", onward
    )

    requests, slot = pl.pallas_call(
        functools.partial(bucket_kernel, nchunk, rows_dev),
        out_shape=[
            jax.ShapeDtypeStruct((nchunk, 128), I32),
            jax.ShapeDtypeStruct((seqs, keys), I32),
        ],
        compiler_params=PARAMS,
    )(neighbour_ids.reshape(seqs, keys))
    slot = lax.ppermute(slot, "group", onward)
    asked = lax.all_to_all(requests, "group", split_axis=0, concat_axis=0, tiled=True)
    weights = round_z(after(pair, asked))
    found = pl.pallas_call(
        functools.partial(fetch_kernel, capacity),
        out_shape=jax.ShapeDtypeStruct((nchunk, capacity * feats), BF),
        compiler_params=PARAMS,
    )(asked, embed_table)
    found = found.reshape(nchunk, 2, -1)
    returned = lax.all_to_all(found, "group", split_axis=0, concat_axis=0, tiled=True)
    returned = after(returned.reshape(nchunk, -1), last_row)
    across_x = mp_size // 2
    along_x = [[2 * x + y for x in range(across_x)] for y in range(2)]
    copies = jax.ShapeDtypeStruct((across_x, id_count, feats), BF)

    def round_x(value):
        return lax.all_to_all(
            value, "mp", split_axis=0, concat_axis=0, tiled=True, axis_index_groups=along_x
        )

    single, encoded = pl.pallas_call(
        functools.partial(order_kernel, capacity),
        out_shape=[jax.ShapeDtypeStruct((id_count, feats), BF), copies],
        compiler_params=PARAMS,
    )(slot, returned)
    single = lax.ppermute(single, "mp", [(m, m ^ 1) for m in range(mp_size)])
    encoded = round_x(encoded)
    encoded_other = round_x(
        pl.pallas_call(copies_kernel, out_shape=copies, compiler_params=PARAMS)(single)
    )

    earlier = jnp.maximum(group_here - 1, 0)
    doc_here = lax.dynamic_slice_in_dim(group_document, group_here, 1, 1)[:, 0]
    doc_before = lax.dynamic_slice_in_dim(group_document, earlier, 1, 1)[:, 0]
    same_doc = (group_here >= 1) & (doc_here == doc_before)
    y_hi = lax.axis_index("mp") % 2
    scalars = jnp.concatenate([y_hi[None].astype(I32), same_doc.astype(I32)])
    whole = lambda *shape: pl.BlockSpec(shape, lambda i, s: (0,) * len(shape))
    kv_part, query = pl.pallas_call(
        functools.partial(project_kernel, run),
        grid_spec=pltpu.PrefetchScalarGridSpec(
            num_scalar_prefetch=1,
            grid=(across_x // 2,),
            in_specs=[
                pl.BlockSpec((2, id_count, feats), lambda i, s: (i, 0, 0)),
                pl.BlockSpec((feats, 2 * cols), lambda i, s: (4 * i + s[0], 0)),
                pl.BlockSpec((feats, 2 * cols), lambda i, s: (4 * i + 2 + s[0], 0)),
                pl.BlockSpec((seqs, length, 4 * feats), lambda i, s: (0, 0, i)),
                pl.BlockSpec((seqs, 4 * feats), lambda i, s: (0, i)),
                pl.BlockSpec((4 * feats, cols), lambda i, s: (i, 2)),
            ],
            out_specs=[whole(id_count, 2 * cols), whole(seqs * length, cols)],
            scratch_shapes=[
                pltpu.VMEM((id_count, 2 * cols), F32),
                pltpu.VMEM((seqs * length, cols), F32),
            ],
        ),
        out_shape=[
            jax.ShapeDtypeStruct((id_count, 2 * cols), F32),
            jax.ShapeDtypeStruct((seqs * length, cols), BF),
        ],
        compiler_params=PARAMS,
    )(scalars, encoded, weights, weights, tokens, last_row, weights)
    att, dquery = pl.pallas_call(
        functools.partial(attend_kernel, run),
        grid_spec=pltpu.PrefetchScalarGridSpec(
            num_scalar_prefetch=1,
            grid=(across_x // 2,),
            in_specs=[
                whole(id_count, 2 * cols),
                whole(seqs * length, cols),
                pl.BlockSpec((2, id_count, feats), lambda i, s: (i, 0, 0)),
                pl.BlockSpec((feats, 2 * cols), lambda i, s: (4 * i + 1 - s[0], 0)),
                pl.BlockSpec((feats, 2 * cols), lambda i, s: (4 * i + 3 - s[0], 0)),
                whole(seqs, length, cols),
                pl.BlockSpec((seqs, cols), lambda i, s: (0, width // cols)),
            ],
            out_specs=[whole(seqs, length, cols), whole(seqs, length, cols)],
            scratch_shapes=[pltpu.VMEM((id_count, 2 * cols), F32)],
        ),
        out_shape=[jax.ShapeDtypeStruct((seqs, length, cols), BF)] * 2,
        compiler_params=PARAMS,
    )(scalars, kv_part, query, encoded_other, weights, weights, attended_grad, last_row)

    last = lax.ppermute(
        jnp.concatenate([att[:, -1], dquery[:, -1]], axis=-1), "group", backward
    )
    fixed = lambda *shape: pl.BlockSpec(shape, lambda i: (0,) * len(shape))
    attended, part = pl.pallas_call(
        functools.partial(token_kernel, run),
        grid=(1,),
        in_specs=[
            fixed(seqs, length, cols),
            fixed(seqs, length, cols),
            fixed(seqs, 2 * cols),
            pl.BlockSpec((width, cols), lambda i: (0, 2)),
        ],
        out_specs=[fixed(seqs, length, cols), fixed(mp_size, seqs * length, feats)],
        out_shape=[
            jax.ShapeDtypeStruct((seqs, length, cols), BF),
            jax.ShapeDtypeStruct((mp_size, seqs * length, feats), BF),
        ],
        compiler_params=PARAMS,
    )(att, dquery, last, weights)
    part = lax.all_to_all(part, "mp", split_axis=0, concat_axis=0, tiled=True)
    part = pl.pallas_call(
        sum_kernel,
        out_shape=jax.ShapeDtypeStruct((mp_size, seqs * length, feats), BF),
        compiler_params=PARAMS,
    )(part)
    part = lax.all_to_all(part, "mp", split_axis=0, concat_axis=0, tiled=True)
    token_grad = pl.pallas_call(
        join_kernel,
        grid=(2,),
        in_specs=[pl.BlockSpec((mp_size // 2, seqs * length, feats), lambda i: (i, 0, 0))],
        out_specs=pl.BlockSpec((seqs * length, width // 2), lambda i: (0, i)),
        out_shape=jax.ShapeDtypeStruct((seqs * length, width), BF),
        compiler_params=PARAMS,
    )(part)
    return (attended, token_grad.reshape(seqs, length, width))


def solution(mesh):
    in_specs = (
        P(None, "group", None),
        P("group", None, None),
        P(),
        P("group", "mp"),
        P("group", "mp"),
        P("group", "mp"),
        P("group", "mp"),
        P(None, "group", "mp"),
    )
    out_specs = (P(None, "group", "mp"), P(None, "group", None))
    return jax.shard_map(local, mesh=mesh, in_specs=in_specs, out_specs=out_specs, check_vma=False)
```
